32 devices in a mesh: groups: 2 (over y), seq: 4 (over z), head: 2 (over x), sub: 2 (over core).
Axes of the slice: x: 2, y: 2, z: 4, core: 2. Of those that a mesh axis runs over, the one named last changes fastest.
Arguments:
- queries: bfloat16 [2816, 64, 128], P(('groups', 'seq'), ('head', 'sub')), parts along dimension 0, may hold values from -0.5 to 0.5
- keys: bfloat16 [2816, 64, 128], P(('groups', 'seq'), ('head', 'sub')), parts along dimension 0, may hold values from -0.5 to 0.5
- values: bfloat16 [2816, 64, 128], P(('groups', 'seq'), ('head', 'sub')), parts along dimension 0, may hold values from -0.625 to 0.625
- output_gradient: bfloat16 [2816, 64, 128], P(('groups', 'seq'), ('head', 'sub')), parts along dimension 0, may hold values from -6 to 6
- decay_exponent: int32 [64], P(('head', 'sub')), may hold values from 5 to 19
- forget_spikes: float32 [2816, 64], P(('groups', 'seq'), ('head', 'sub')), parts along dimension 0, may hold values from 0 to 0.69
Outputs:
- query_grad: bfloat16 [2816, 64, 128], P(('groups', 'seq'), ('head', 'sub')), parts along dimension 0
- key_grad: bfloat16 [2816, 64, 128], P(('groups', 'seq'), ('head', 'sub')), parts along dimension 0
- value_grad: bfloat16 [2816, 64, 128], P(('groups', 'seq'), ('head', 'sub')), parts along dimension 0
The draws below stay inside these ranges and needn't reach their ends.
There are 2 independent parts, one for each index of `groups`. The reference program is written for one: setup_inputs(seed, part) draws one part's arguments, and reference() takes and returns one part's arrays. A program takes and returns all parts, laid end to end along the dimension named above; an argument that names none is the same for every part. Nothing has to cross between parts.
All inputs are finite; a program needn't handle non-finite values.
Results may differ from the reference program's by a relative error of at most 0.0075.
Values may be sent and summed in bfloat16 or wider, within the bound.
No kernel may reach another device: no remote copies, remote signals or barrier semaphores. Data moves between devices by JAX's collectives and lax.ppermute only.
A program may use at most 128 MiB of HBM per device.

```python
import jax
import jax.numpy as jnp
from jax import lax

HEAD_COUNT = 64
DH = 128
SPAN_TOKENS = 352
SEQ = 1408
N_SEQ = 4


def draw_forget_spikes(key, part):
    key = jax.random.fold_in(key, 7)
    place_key, size_key = jax.random.split(key)
    places = jax.random.randint(place_key, (4, HEAD_COUNT), 0, SEQ)
    strength = jax.random.uniform(size_key, (4, HEAD_COUNT), jnp.float32, 0.22, 0.69)
    tokens_at = jnp.arange(SEQ)[None, :, None]
    struck = jnp.where(tokens_at == places[:, None, :], strength[:, None, :], 0.0)
    return jnp.max(struck, axis=0)


def plant(entries, key, smallest, largest):
    place = [jax.random.randint(jax.random.fold_in(key, axis), (), 0, length) for axis, length in enumerate(entries.shape)]
    main_axis = entries.shape.index(max(entries.shape))
    beside = place[:main_axis] + [(place[main_axis] + 1) % entries.shape[main_axis]] + place[main_axis + 1:]
    return entries.at[tuple(place)].set(smallest).at[tuple(beside)].set(largest)


def shard_levels(key, shape, cuts, low, largest):
    def one(dim, parts):
        heights = jax.random.uniform(jax.random.fold_in(jax.random.fold_in(key, 6), dim), (parts,), jnp.float32, low / len(cuts), largest / len(cuts))
        return jnp.repeat(jnp.exp(heights), shape[dim] // parts).reshape((-1,) + (1,) * (len(shape) - dim - 1))

    gain = one(*cuts[0])
    for cut in cuts[1:]:
        gain = gain * one(*cut)
    return gain


def noise(key, shape, width, most, shards=(), held_as=jnp.bfloat16):
    values = width * jax.random.normal(key, shape, jnp.float32)
    if shards:
        values = values * shard_levels(key, shape, shards, -0.22, 0.18)
    return jnp.clip(values, -most, most).astype(held_as)


def setup_inputs(seed: int = 0, part: int = 0) -> dict:
    key_list = jax.random.split(jax.random.key(seed), 7)
    part_splits = jax.random.split(jax.random.fold_in(key_list[6], part), 7)
    return {
        "queries": noise(part_splits[0], (SEQ, HEAD_COUNT, DH), (DH ** -0.5), 0.5, ((0, 4), (1, 4))),
        "keys": noise(part_splits[1], (SEQ, HEAD_COUNT, DH), (DH ** -0.5), 0.5, ((0, 4), (1, 4))),
        "values": noise(part_splits[2], (SEQ, HEAD_COUNT, DH), 0.1, 0.625, ((0, 4), (1, 4))),
        "output_gradient": noise(part_splits[3], (SEQ, HEAD_COUNT, DH), 1.0, 6.0, ((0, 4), (1, 4))),
        "decay_exponent": plant(jax.random.randint(key_list[4], (HEAD_COUNT,), 5, 20), jax.random.fold_in(key_list[4], 1), 5, 19).astype(jnp.int32),
        "forget_spikes": draw_forget_spikes(jax.random.fold_in(jax.random.fold_in(key_list[6], part), 71), part),
    }


def rounded(tensor):
    return lax.optimization_barrier(tensor.astype(jnp.bfloat16)).astype(jnp.float32)


def forget_parts(decay_exponent, forget_spikes):
    forget_logs = jnp.exp2(-decay_exponent.astype(jnp.float32))[None, :] + forget_spikes
    inside_span = jnp.cumsum(forget_logs, axis=0)
    whole_span_decay = inside_span[-1]
    entry_decay = jnp.exp(-inside_span)
    exit_decay = jnp.exp(-(whole_span_decay[None, :] - inside_span))
    return inside_span, whole_span_decay, entry_decay, exit_decay


def reduce_spans(queries, keys, values, output_gradient, decay_exponent, forget_spikes):
    inside_span, whole_span_decay, entry_decay, exit_decay = forget_parts(decay_exponent, forget_spikes)
    key_out = rounded(keys.astype(jnp.float32) * exit_decay[:, :, None])
    query_in = rounded(queries.astype(jnp.float32) * entry_decay[:, :, None])
    kv_sum = rounded(jnp.einsum("thd,the->hde", key_out, values.astype(jnp.float32), precision=lax.Precision.HIGHEST))
    grad_sum = rounded(jnp.einsum("thd,the->hde", query_in, output_gradient.astype(jnp.float32), precision=lax.Precision.HIGHEST))
    return kv_sum, grad_sum, jnp.exp(-whole_span_decay)


def input_gradients(queries, keys, values, output_gradient, decay_exponent, forget_spikes, leading_state, trailing_state):
    inside_span, whole_span_decay, entry_decay, exit_decay = forget_parts(decay_exponent, forget_spikes)
    length = inside_span.shape[0]
    causal = jnp.arange(length)[:, None] >= jnp.arange(length)[None, :]
    spread = inside_span.T[:, :, None] - inside_span.T[:, None, :]
    weight = jnp.where(causal[None], jnp.exp(-jnp.maximum(spread, 0.0)), 0.0)
    query_f = queries.astype(jnp.float32)
    key_f = keys.astype(jnp.float32)
    value_f = values.astype(jnp.float32)
    grad_f = output_gradient.astype(jnp.float32)
    highest = lax.Precision.HIGHEST
    scores = jnp.einsum("thd,shd->hts", query_f, key_f, precision=highest)
    probes = jnp.einsum("the,she->hts", grad_f, value_f, precision=highest)
    masked_scores = rounded(scores * weight)
    masked_probes = rounded(probes * weight)
    prefix_r = rounded(leading_state)
    suffix_r = rounded(trailing_state)
    query_grad = jnp.einsum("hts,shd->thd", masked_probes, key_f, precision=highest) + entry_decay[:, :, None] * jnp.einsum("the,hde->thd", grad_f, prefix_r, precision=highest)
    key_grad = jnp.einsum("hts,thd->shd", masked_probes, query_f, precision=highest) + exit_decay[:, :, None] * jnp.einsum("she,hde->shd", value_f, suffix_r, precision=highest)
    value_grad = jnp.einsum("hts,the->she", masked_scores, grad_f, precision=highest) + exit_decay[:, :, None] * jnp.einsum("shd,hde->she", key_f, suffix_r, precision=highest)
    return query_grad.astype(jnp.bfloat16), key_grad.astype(jnp.bfloat16), value_grad.astype(jnp.bfloat16)


def reference(queries, keys, values, output_gradient, decay_exponent, forget_spikes):
    array_dims = (N_SEQ, SPAN_TOKENS, HEAD_COUNT, DH)
    token_blocks = (queries.reshape(array_dims), keys.reshape(array_dims), values.reshape(array_dims), output_gradient.reshape(array_dims), forget_spikes.reshape(N_SEQ, SPAN_TOKENS, HEAD_COUNT))
    kv_sums, grad_sums, span_fades = lax.map(lambda inputs: reduce_spans(inputs[0], inputs[1], inputs[2], inputs[3], decay_exponent, inputs[4]), token_blocks)

    def advance(state, inputs):
        fade_now, term = inputs
        return fade_now[:, None, None] * state + term, state

    zero_state = jnp.zeros((HEAD_COUNT, DH, DH), jnp.float32)
    _, prefixes = lax.scan(advance, zero_state, (span_fades, kv_sums))
    _, suffixes = lax.scan(advance, zero_state, (span_fades, grad_sums), reverse=True)
    query_grad, key_grad, value_grad = lax.map(lambda inputs: input_gradients(inputs[0], inputs[1], inputs[2], inputs[3], decay_exponent, inputs[4], inputs[5], inputs[6]), token_blocks + (prefixes, suffixes))
    return (query_grad.reshape(SEQ, HEAD_COUNT, DH), key_grad.reshape(SEQ, HEAD_COUNT, DH), value_grad.reshape(SEQ, HEAD_COUNT, DH))
```

```python
import functools

import jax
import jax.numpy as jnp
from jax import lax
from jax.experimental import pallas as pl
from jax.experimental.pallas import tpu as pltpu
from jax.sharding import PartitionSpec as P

VMEM = pl.BlockSpec(memory_space=pltpu.VMEM)
SMEM = pl.BlockSpec(memory_space=pltpu.SMEM)
ANY = pl.BlockSpec(memory_space=pl.ANY)
BF16, F32 = jnp.bfloat16, jnp.float32
NT = (((1,), (1,)), ((), ()))
TN = (((0,), (0,)), ((), ()))
NN = (((1,), (0,)), ((), ()))
UNROLL = 4
MIB = 2**20


def dot(a, b, dims=NN):
    return lax.dot_general(a, b, dims, preferred_element_type=F32)


def running_forget(decay, spikes):
    heads, length = spikes.shape
    wide = -(-length // 128) * 128
    head = lax.broadcasted_iota(jnp.int32, (heads, 1), 0)
    exponent = jnp.zeros((heads, 1), jnp.int32)
    for h in range(heads):
        exponent = jnp.where(head == h, decay[h], exponent)
    forget = jnp.exp2(-exponent.astype(F32)) + spikes[...]
    if wide > length:
        forget = jnp.concatenate([forget, jnp.zeros((heads, wide - length), F32)], axis=1)
    lane = lax.broadcasted_iota(jnp.int32, forget.shape, 1)
    step = 1
    while step < length:
        forget = forget + jnp.where(lane >= step, pltpu.roll(forget, step, 1), 0.0)
        step *= 2
    return forget


def column_of(columns, h, length):
    return jnp.broadcast_to(columns[:length, h : h + 1], (length, 128))


def kv_sum_of(k, v, column):
    leave = jnp.exp(column - column[-1:])
    return dot((k.astype(F32) * leave).astype(BF16), v, TN).astype(BF16)


def grad_sum_of(q, g, column):
    return dot((q.astype(F32) * jnp.exp(-column)).astype(BF16), g, TN).astype(BF16)


def first_kernel(count, heads, decay, spikes, q, k, v, g, payload, left, right, sems):
    place = lax.axis_index("seq")
    length = spikes.shape[1]

    def run(a, b, sum_of):
        copies = [
            pltpu.make_async_copy(a, left, sems.at[0]),
            pltpu.make_async_copy(b, right, sems.at[1]),
        ]
        for copy in copies:
            copy.start()
        columns = running_forget(decay, spikes).T
        for copy in copies:
            copy.wait()
        a_h = jnp.swapaxes(left[:, :heads, :], 0, 1)
        b_h = jnp.swapaxes(right[:, :heads, :], 0, 1)
        for h in range(heads):
            payload[h] = sum_of(a_h[h], b_h[h], column_of(columns, h, length))

    @pl.when(place == 0)
    def _():
        run(k, v, kv_sum_of)

    @pl.when(place == count - 1)
    def _():
        run(q, g, grad_sum_of)


def sums_kernel(
    count, heads, decay, spikes, q, k, v, g, qh, kh, vh, gh, col, row, kv, grad, fade, *payloads
):
    all_heads, length = spikes.shape
    place = lax.axis_index("seq")
    within = running_forget(decay, spikes)
    row[...] = within[:, None, :]
    fade[...] = jnp.broadcast_to(jnp.exp(-within[:, length - 1 : length])[:, :, None], fade.shape)
    columns = within.T
    for h in range(all_heads):
        col[h] = column_of(columns, h, length)
    kh[...] = jnp.swapaxes(k[...], 0, 1)
    vh[...] = jnp.swapaxes(v[...], 0, 1)

    @pl.when(place < count - 1)
    def _():
        for h in range(all_heads):
            kv[h] = kv_sum_of(kh[h], vh[h], col[h])

    qh[...] = jnp.swapaxes(q[...], 0, 1)
    gh[...] = jnp.swapaxes(g[...], 0, 1)

    @pl.when(place > 0)
    def _():
        for h in range(all_heads):
            grad[h] = grad_sum_of(qh[h], gh[h], col[h])

    for i, payload in enumerate(payloads):
        start = (i + 1) * heads

        @pl.when(place == 0)
        def _():
            payload[...] = kv[start : start + heads]

        @pl.when(place == count - 1)
        def _():
            payload[...] = grad[start : start + heads]


def merge_kernel(count, hop, start, got, kv, grad, fade, payload):
    place = lax.axis_index("seq")
    heads = got.shape[0]
    cut = slice(start, start + heads)
    for at, own in ((hop, kv), (count - 1 - hop, grad)):

        @pl.when(place == at)
        def _():
            payload[...] = (fade[cut] * got[...].astype(F32) + own[cut].astype(F32)).astype(BF16)


def intra_kernel(start, col, row, qh, kh, vh, gh, qg, kg, vg):
    heads, length, _ = qg.shape
    edges = list(range(0, length, 256)) + [length]
    blocks = list(zip(edges[:-1], edges[1:]))

    def one(i, carry):
        h = start + i
        q, k, v, g = qh[h], kh[h], vh[h], gh[h]
        qt, gt = q.T, g.T
        scores, probes = {}, {}
        for t0, t1 in blocks:
            for s0, s1 in blocks:
                if s0 > t0:
                    continue
                column = col[h, t0:t1, :]
                if s1 - s0 > 128:
                    column = jnp.concatenate([column, column], axis=1)
                spread = row[h, :, s0:s1] - column[:, : s1 - s0]
                weight = jnp.exp(jnp.minimum(spread, 0.0))
                if s0 == t0:
                    t = lax.broadcasted_iota(jnp.int32, spread.shape, 0)
                    s = lax.broadcasted_iota(jnp.int32, spread.shape, 1)
                    weight = jnp.where(t >= s, weight, 0.0)
                scores[t0, s0] = (dot(q[t0:t1], k[s0:s1], NT) * weight).astype(BF16)
                probes[t0, s0] = (dot(g[t0:t1], v[s0:s1], NT) * weight).astype(BF16)
        for t0, t1 in blocks:
            qg[i, t0:t1, :] = sum(dot(probes[t0, s0], k[s0:s1]) for s0, s1 in blocks if s0 <= t0)
        for s0, s1 in blocks:
            after = [(t0, t1) for t0, t1 in blocks if t0 >= s0]
            kg[i, s0:s1, :] = sum(dot(qt[:, t0:t1], probes[t0, s0]) for t0, t1 in after).T
            vg[i, s0:s1, :] = sum(dot(gt[:, t0:t1], scores[t0, s0]) for t0, t1 in after).T
        return carry

    lax.fori_loop(0, heads, one, 0, unroll=min(UNROLL, heads))


def final_kernel(count, chunks, last, col, kh, vh, gh, *rest):
    hops = 1 if last else count - 2
    intra, rest = rest[: 3 * chunks], rest[3 * chunks :]
    arrived, rest = rest[: hops * chunks], rest[hops * chunks :]
    if last:
        rest = rest[3:]
    outs, (state, by_head, tokens, sems) = rest[:3], rest[3:]
    all_heads, length, _ = kh.shape
    heads = all_heads // chunks
    place = lax.axis_index("seq")

    def take(from_hop):
        for hop in [count - 1] if last else range(1, count - 1):

            @pl.when(place == from_hop(hop))
            def _():
                for c in range(chunks):
                    state[c * heads : (c + 1) * heads] = arrived[c * hops + (0 if last else hop - 1)][...]

    def write(j, term):
        for c in range(chunks):

            def one(i, carry):
                h = c * heads + i
                by_head[j, h] = (intra[3 * c + j][i] + term(h)).astype(BF16)
                return carry

            lax.fori_loop(0, heads, one, 0, unroll=min(UNROLL, heads))
        tokens[j] = jnp.swapaxes(by_head[j], 0, 1)
        pltpu.make_async_copy(tokens.at[j], outs[j], sems.at[j]).start()

    def wait(j):
        pltpu.make_async_copy(tokens.at[j], outs[j], sems.at[j]).wait()

    def enter(h):
        return jnp.exp(-col[h])

    def leave(h):
        return jnp.exp(col[h] - col[h, length - 1 : length, :])

    does_q = place == count - 1 if last else place < count - 1
    does_kv = place == 0 if last else place > 0

    @pl.when(does_q)
    def _():
        if not last:

            @pl.when(place == 0)
            def _():
                state[...] = jnp.zeros_like(state)

        take(lambda hop: hop)
        write(0, lambda h: enter(h) * dot(gh[h], state[h], NT))

    @pl.when(does_kv)
    def _():
        if not last:

            @pl.when(place == count - 1)
            def _():
                state[...] = jnp.zeros_like(state)

        take(lambda hop: count - 1 - hop)
        write(1, lambda h: leave(h) * dot(vh[h], state[h], NT))
        write(2, lambda h: leave(h) * dot(kh[h], state[h]))

    @pl.when(does_q)
    def _():
        wait(0)

    @pl.when(does_kv)
    def _():
        wait(1)
        wait(2)


def per_device(count, queries, keys, values, output_gradient, decay_exponent, forget_spikes):
    length, all_heads, size = queries.shape
    heads = 8 if all_heads % 8 == 0 else all_heads
    chunks = all_heads // heads
    spikes = forget_spikes.T
    shape = jax.ShapeDtypeStruct
    wide = -(-length // 128) * 128
    by_head = shape((all_heads, length, size), BF16)
    by_head_f = shape((all_heads, length, size), F32)
    part_f = shape((heads, length, size), F32)
    states = shape((all_heads, size, size), BF16)
    state = shape((heads, size, size), BF16)
    flops = 2 * heads * length * size * size

    def call(kernel, outs, n_in, limit, n, nbytes, specs=None, **more):
        return pl.pallas_call(
            kernel,
            out_shape=outs,
            in_specs=specs or [VMEM] * n_in,
            compiler_params=pltpu.CompilerParams(vmem_limit_bytes=limit * MIB),
            cost_estimate=pl.CostEstimate(flops=n * flops, bytes_accessed=nbytes, transcendentals=0),
            **more,
        )

    tensors = (queries, keys, values, output_gradient)
    raw = pltpu.VMEM(queries.shape, BF16)
    first = call(
        functools.partial(first_kernel, count, heads),
        state,
        6,
        60,
        1,
        3 << 20,
        specs=[SMEM, VMEM] + [ANY] * 4,
        out_specs=VMEM,
        scratch_shapes=[raw, raw, pltpu.SemaphoreType.DMA((2,))],
    )(decay_exponent, spikes, *tensors)
    qh, kh, vh, gh, col, row, kv, grad, fade, *others = call(
        functools.partial(sums_kernel, count, heads),
        (by_head,) * 4
        + (by_head_f, shape((all_heads, 1, wide), F32), states, states)
        + (shape((all_heads, 1, size), F32),)
        + (state,) * (chunks - 1),
        6,
        8,
        4,
        8 << 20,
        specs=[SMEM] + [VMEM] * 5,
        out_specs=(VMEM,) * (9 + chunks - 1),
    )(decay_exponent, spikes, *tensors)

    payloads = [first, *others]
    arrived = [[] for _ in range(chunks)]
    for hop in range(1, count):
        pairs = [(hop - 1, hop), (count - hop, count - hop - 1)]
        for c in range(chunks):
            got = lax.ppermute(payloads[c], "seq", pairs)
            arrived[c].append(got)
            if hop < count - 1:
                payloads[c] = call(
                    functools.partial(merge_kernel, count, hop, c * heads),
                    state,
                    4,
                    4,
                    0,
                    1 << 20,
                    out_specs=VMEM,
                )(got, kv, grad, fade)
    intra = []
    for c in range(chunks):
        intra += call(
            functools.partial(intra_kernel, c * heads), (part_f,) * 3, 6, 8, 14, 4 << 20, out_specs=(VMEM,) * 3
        )(col, row, qh, kh, vh, gh)

    full = shape(queries.shape, BF16)

    def finish(last, outs):
        hops = 1 if last else count - 2
        came = [a for c in range(chunks) for a in (arrived[c][-1:] if last else arrived[c][:-1])]
        fixed = 4 + 3 * chunks + len(came)
        return call(
            functools.partial(final_kernel, count, chunks, last),
            (full,) * 3,
            fixed,
            16,
            3,
            8 << 20,
            specs=[VMEM] * fixed + [ANY] * len(outs),
            out_specs=(ANY,) * 3,
            scratch_shapes=[
                pltpu.VMEM(states.shape, BF16),
                pltpu.VMEM((3,) + by_head.shape, BF16),
                pltpu.VMEM((3,) + full.shape, BF16),
                pltpu.SemaphoreType.DMA((3,)),
            ],
            input_output_aliases={fixed + j: j for j in range(len(outs))},
        )(col, kh, vh, gh, *intra, *came, *outs)

    return tuple(finish(True, finish(False, ())))


def solution(mesh):
    tokens = P(("groups", "seq"), ("head", "sub"), None)
    in_specs = (tokens,) * 4 + (P(("head", "sub")), P(("groups", "seq"), ("head", "sub")))
    return jax.shard_map(
        functools.partial(per_device, mesh.shape["seq"]),
        mesh=mesh,
        in_specs=in_specs,
        out_specs=(tokens,) * 3,
        check_vma=False,
    )
```

```python
import functools

import jax
import jax.numpy as jnp
from jax import lax
from jax.experimental import pallas as pl
from jax.experimental.pallas import tpu as pltpu
from jax.sharding import PartitionSpec as P

VMEM = pl.BlockSpec(memory_space=pltpu.VMEM)
ANY = pl.BlockSpec(memory_space=pl.ANY)
BF16, F32 = jnp.bfloat16, jnp.float32
NT = (((1,), (1,)), ((), ()))
TN = (((0,), (0,)), ((), ()))
NN = (((1,), (0,)), ((), ()))
UNROLL = 4
CHUNKS = 3
DUE = {(0, 0): 5, (2, 1): 9}
MIB = 2**20
TOKEN = jax.ShapeDtypeStruct((8, 128), F32)


def dot(a, b, dims=NN):
    return lax.dot_general(a, b, dims, preferred_element_type=F32)


def running_forget(decay, spikes):
    heads, length = spikes.shape
    wide = -(-length // 128) * 128
    same = lax.broadcasted_iota(jnp.int32, (heads, heads), 0) == lax.broadcasted_iota(jnp.int32, (heads, heads), 1)
    exponent = jnp.sum(jnp.where(same, decay[...].astype(F32), 0.0), axis=1, keepdims=True)
    forget = jnp.exp2(-exponent) + spikes[...]
    if wide > length:
        forget = jnp.concatenate([forget, jnp.zeros((heads, wide - length), F32)], axis=1)
    lane = lax.broadcasted_iota(jnp.int32, forget.shape, 1)
    step = 1
    while step < length:
        forget = forget + jnp.where(lane >= step, pltpu.roll(forget, step, 1), 0.0)
        step *= 2
    return forget


def state_sum(left, right, fade):
    return dot((left.T.astype(F32) * fade).astype(BF16), right).astype(BF16)


def enter_of(within, h, length):
    return jnp.exp(-within[h : h + 1, :length])


def leave_of(within, h, length):
    return jnp.exp(within[h : h + 1, :length] - within[h : h + 1, length - 1 : length])


def first_kernel(count, heads, decay, spikes, q, k, v, g, *rest):
    payloads, (_, decay_v, spikes_v, left, right, sems) = rest[-6 - len(heads) : -6], rest[-6:]
    place = lax.axis_index("seq")
    length = spikes.shape[1]

    def run(a, b, fade_of):
        copies = [
            pltpu.make_async_copy(source, target, sems.at[i])
            for i, (source, target) in enumerate(
                ((spikes, spikes_v), (decay, decay_v), (a, left), (b, right))
            )
        ]
        for copy in copies:
            copy.start()
        for copy in copies[:2]:
            copy.wait()
        within = running_forget(decay_v, spikes_v)
        fades = {h: fade_of(within, h, length) for part in heads for h in part}
        for copy in copies[2:]:
            copy.wait()
        a_h = jnp.swapaxes(left[...], 0, 1)
        b_h = jnp.swapaxes(right[...], 0, 1)
        for part, payload in zip(heads, payloads):
            for i, h in enumerate(part):
                payload[i] = state_sum(a_h[h], b_h[h], fades[h])

    @pl.when(place == 0)
    def _():
        run(k, v, leave_of)

    @pl.when(place == count - 1)
    def _():
        run(q, g, enter_of)


def sums_kernel(count, decay, spikes, q, k, v, g, *rest):
    qh, kh, vh, gh, col, row, kv, grad, fade = rest[-9:]
    all_heads, length = spikes.shape
    place = lax.axis_index("seq")
    within = running_forget(decay, spikes)
    row[...] = within[:, None, :]
    fade[...] = jnp.broadcast_to(jnp.exp(-within[:, length - 1 : length])[:, :, None], fade.shape)
    kh[...] = jnp.swapaxes(k[...], 0, 1)
    vh[...] = jnp.swapaxes(v[...], 0, 1)
    qh[...] = jnp.swapaxes(q[...], 0, 1)
    gh[...] = jnp.swapaxes(g[...], 0, 1)

    @pl.when((place > 0) & (place < count - 1))
    def _():
        for h in range(all_heads):
            kv[h] = state_sum(kh[h], vh[h], leave_of(within, h, length))
            grad[h] = state_sum(qh[h], gh[h], enter_of(within, h, length))

    columns = within.T
    for h in range(all_heads):
        col[h] = jnp.broadcast_to(columns[:length, h : h + 1], (length, 128))


def merge_kernel(count, hop, start, got, kv, grad, fade, *rest):
    payload = rest[-2]
    place = lax.axis_index("seq")
    heads = got.shape[0]
    cut = slice(start, start + heads)
    for at, own in ((hop, kv), (count - 1 - hop, grad)):

        @pl.when(place == at)
        def _():
            payload[...] = (fade[cut] * got[...].astype(F32) + own[cut].astype(F32)).astype(BF16)


def intra_kernel(start, heads, col, row, qh, kh, vh, gh, *rest):
    qg, kg, vg = rest[-4:-1]
    length = qh.shape[1]
    edges = list(range(0, length, 256)) + [length]
    blocks = list(zip(edges[:-1], edges[1:]))

    def one(h, carry):
        q, k, v, g = qh[h], kh[h], vh[h], gh[h]
        qt, gt = q.T, g.T
        scores, probes = {}, {}
        for t0, t1 in blocks:
            for s0, s1 in blocks:
                if s0 > t0:
                    continue
                column = col[h, t0:t1, :]
                if s1 - s0 > 128:
                    column = jnp.concatenate([column, column], axis=1)
                spread = row[h, :, s0:s1] - column[:, : s1 - s0]
                weight = jnp.exp(jnp.minimum(spread, 0.0))
                if s0 == t0:
                    t = lax.broadcasted_iota(jnp.int32, spread.shape, 0)
                    s = lax.broadcasted_iota(jnp.int32, spread.shape, 1)
                    weight = jnp.where(t >= s, weight, 0.0)
                scores[t0, s0] = (dot(q[t0:t1], k[s0:s1], NT) * weight).astype(BF16)
                probes[t0, s0] = (dot(g[t0:t1], v[s0:s1], NT) * weight).astype(BF16)
        for t0, t1 in blocks:
            qg[h, t0:t1, :] = sum(dot(probes[t0, s0], k[s0:s1]) for s0, s1 in blocks if s0 <= t0)
        for s0, s1 in blocks:
            after = [(t0, t1) for t0, t1 in blocks if t0 >= s0]
            kg[h, s0:s1, :] = sum(dot(qt[:, t0:t1], probes[t0, s0]) for t0, t1 in after).T
            vg[h, s0:s1, :] = sum(dot(gt[:, t0:t1], scores[t0, s0]) for t0, t1 in after).T
        return carry

    lax.fori_loop(start, start + heads, one, 0, unroll=min(UNROLL, heads))


def terms(col, kh, vh, gh, state, start, h):
    length = kh.shape[1]

    def leave():
        return jnp.exp(col[h] - col[h, length - 1 : length, :])

    return (
        lambda: jnp.exp(-col[h]) * dot(gh[h], state[h - start], NT),
        lambda: leave() * dot(vh[h], state[h - start], NT),
        lambda: leave() * dot(kh[h], state[h - start]),
    )


def add_terms(which, target, slot, intra, col, kh, vh, gh, state, start, heads):
    def one(i, carry):
        h = start + i
        target[slot, i] = (intra[which][h] + terms(col, kh, vh, gh, state, start, h)[which]()).astype(BF16)
        return carry

    lax.fori_loop(0, heads, one, 0, unroll=min(2 * UNROLL, heads))


def out_copies(tokens, out, sem, parts=2):
    step = tokens.shape[0] // parts
    cuts = [slice(i * step, (i + 1) * step) for i in range(parts)]
    return [(cut, pltpu.make_async_copy(tokens.at[cut], out.at[cut], sem.at[i])) for i, cut in enumerate(cuts)]


def send_out(by_head, tokens, out, sem):
    for cut, copy in out_copies(tokens, out, sem):
        tokens[cut] = jnp.swapaxes(by_head[:, cut, :], 0, 1)
        copy.start()


def wait_out(tokens, out, sem):
    for _, copy in out_copies(tokens, out, sem):
        copy.wait()


def between_kernel(count, sizes, col, kh, vh, gh, qg, kg, vg, *rest):
    hops, chunks = count - 2, len(sizes)
    arrived = rest[: hops * chunks]
    *outs, state, by_head, tokens, sems = rest[-7:]
    intra = (qg, kg, vg)
    all_heads = kh.shape[0]
    place = lax.axis_index("seq")

    def take(end, came_from):
        @pl.when(place == end)
        def _():
            state[...] = jnp.zeros_like(state)

        for hop in range(1, count - 1):

            @pl.when(place == came_from(hop))
            def _():
                at = 0
                for c, heads in enumerate(sizes):
                    state[at : at + heads] = arrived[c * hops + hop - 1][...]
                    at += heads

    def write(which):
        add_terms(which, by_head, which, intra, col, kh, vh, gh, state, 0, all_heads)
        send_out(by_head[which], tokens.at[which], outs[which], sems.at[which])

    @pl.when(place < count - 1)
    def _():
        take(0, lambda hop: hop)
        write(0)

    @pl.when(place > 0)
    def _():
        take(count - 1, lambda hop: count - 1 - hop)
        write(1)
        write(2)

    @pl.when(place < count - 1)
    def _():
        wait_out(tokens.at[0], outs[0], sems.at[0])

    @pl.when(place > 0)
    def _():
        wait_out(tokens.at[1], outs[1], sems.at[1])
        wait_out(tokens.at[2], outs[2], sems.at[2])


def ends_kernel(count, start, col, kh, vh, gh, qg, kg, vg, got, *rest):
    by_head = rest[-1]
    heads = got.shape[0]
    place = lax.axis_index("seq")
    args = ((qg, kg, vg), col, kh, vh, gh, got, start, heads)

    @pl.when(place == count - 1)
    def _():
        add_terms(0, by_head, 0, *args)

    @pl.when(place == 0)
    def _():
        add_terms(1, by_head, 0, *args)
        add_terms(2, by_head, 1, *args)


def last_kernel(count, start, col, kh, vh, gh, qg, kg, vg, got, *rest):
    *outs, by_head, tokens, sems = rest[-6:]
    earlier = rest[:-9]
    heads = got.shape[0]
    place = lax.axis_index("seq")
    args = ((qg, kg, vg), col, kh, vh, gh, got, start, heads)

    def write(which, slot):
        add_terms(which, by_head, slot, *args)
        whole = jnp.concatenate([part[slot] for part in earlier] + [by_head[slot]], axis=0)
        send_out(whole, tokens.at[slot], outs[which], sems.at[slot])

    @pl.when(place == count - 1)
    def _():
        write(0, 0)
        wait_out(tokens.at[0], outs[0], sems.at[0])

    @pl.when(place == 0)
    def _():
        write(1, 0)
        write(2, 1)
        wait_out(tokens.at[0], outs[1], sems.at[0])
        wait_out(tokens.at[1], outs[2], sems.at[1])


def per_device(count, queries, keys, values, output_gradient, decay_exponent, forget_spikes):
    length, all_heads, size = queries.shape
    chunks = CHUNKS
    sizes = [all_heads // chunks + (c < all_heads % chunks) for c in range(chunks)]
    starts = [sum(sizes[:c]) for c in range(chunks)]
    spikes = forget_spikes.T
    shape = jax.ShapeDtypeStruct
    wide = -(-length // 128) * 128
    by_head = shape((all_heads, length, size), BF16)
    by_head_f = shape((all_heads, length, size), F32)
    states = shape((all_heads, size, size), BF16)
    full = shape(queries.shape, BF16)
    flops = 2 * length * size * size

    def state(c):
        return shape((sizes[c], size, size), BF16)

    def call(kernel, ins, outs, limit, cost, after=(), specs=None, out_spec=VMEM, **more):
        several = isinstance(outs, tuple)
        return pl.pallas_call(
            kernel,
            out_shape=outs,
            in_specs=(specs or [VMEM] * len(ins)) + [ANY] * len(after),
            out_specs=tuple(ANY if o is TOKEN else out_spec for o in outs) if several else out_spec,
            compiler_params=pltpu.CompilerParams(vmem_limit_bytes=limit * MIB),
            cost_estimate=pl.CostEstimate(flops=cost * flops, bytes_accessed=1 << 20, transcendentals=0),
            **more,
        )(*ins, *after)

    tensors = (queries, keys, values, output_gradient)
    raw = pltpu.VMEM(queries.shape, BF16)
    decay = decay_exponent[None, :]
    ranges = [range(a, a + n) for a, n in zip(starts, sizes)]
    payloads = []
    for part in (slice(0, 1), slice(1, chunks)):
        *several, token = call(
            functools.partial(first_kernel, count, ranges[part]),
            (decay, spikes, *tensors),
            (*(state(c) for c in range(chunks)[part]), TOKEN),
            52 if payloads else 60,
            sum(sizes[part]),
            specs=[ANY] * 6,
            scratch_shapes=[
                pltpu.VMEM(decay.shape, jnp.int32),
                pltpu.VMEM(spikes.shape, F32),
                raw,
                raw,
                pltpu.SemaphoreType.DMA((4,)),
            ],
        )
        payloads += several
    qh, kh, vh, gh, col, row, kv, grad, fade = call(
        functools.partial(sums_kernel, count),
        (decay, spikes, *tensors),
        (by_head,) * 4
        + (by_head_f, shape((all_heads, 1, wide), F32), states, states)
        + (shape((all_heads, 1, size), F32),),
        8,
        2 * all_heads,
        after=(token,),
    )

    intra, placed, done, merged = [], 0, (), ()
    ins = (col, row, qh, kh, vh, gh)

    def span_products(hop, chunk, before=None):
        nonlocal intra, placed, done
        due = all_heads if before is None else all_heads * DUE.get((hop, chunk), 0) // 16
        if due > placed:
            *intra, token = call(
                functools.partial(intra_kernel, placed, due - placed),
                (*ins, *intra),
                (by_head_f,) * 3 + (TOKEN,),
                8,
                5 * (due - placed),
                after=merged if before is None else before,
                input_output_aliases={len(ins) + j: j for j in range(len(intra))},
            )
            placed, done = due, (token,)

    arrived = [[] for _ in range(chunks)]
    span_products(0, 0, ())
    for hop in range(1, count):
        pairs = [(hop - 1, hop), (count - hop, count - hop - 1)]
        for c in range(chunks):
            got = lax.ppermute(payloads[c], "seq", pairs)
            arrived[c].append(got)
            if hop < count - 1:
                payloads[c], *merged = call(
                    functools.partial(merge_kernel, count, hop, starts[c]),
                    (got, kv, grad, fade),
                    (state(c), TOKEN),
                    4,
                    0,
                    after=done,
                )
                done = ()
                span_products(hop, c, merged)
    span_products(0, 0)

    common = (col, kh, vh, gh, *intra)
    came = [a for c in range(chunks) for a in arrived[c][:-1]]
    outs = call(
        functools.partial(between_kernel, count, sizes),
        (*common, *came),
        (full,) * 3,
        16,
        3 * all_heads,
        after=merged,
        out_spec=ANY,
        scratch_shapes=[
            pltpu.VMEM(states.shape, BF16),
            pltpu.VMEM((3,) + by_head.shape, BF16),
            pltpu.VMEM((3,) + full.shape, BF16),
            pltpu.SemaphoreType.DMA((3, 2)),
        ],
    )
    earlier = []
    for c in range(chunks - 1):
        earlier.append(
            call(
                functools.partial(ends_kernel, count, starts[c]),
                (*common, arrived[c][-1]),
                shape((2, sizes[c], length, size), BF16),
                8,
                2 * sizes[c],
                after=earlier[-1:],
            )
        )
    ins = (*common, arrived[-1][-1], *earlier)
    return tuple(
        call(
            functools.partial(last_kernel, count, starts[-1]),
            (*ins, *outs),
            (full,) * 3,
            8,
            2 * sizes[-1],
            specs=[VMEM] * len(ins) + [ANY] * 3,
            out_spec=ANY,
            scratch_shapes=[
                pltpu.VMEM((2, sizes[-1], length, size), BF16),
                pltpu.VMEM((2,) + full.shape, BF16),
                pltpu.SemaphoreType.DMA((2, 2)),
            ],
            input_output_aliases={len(ins) + j: j for j in range(3)},
        )
    )


def solution(mesh):
    tokens = P(("groups", "seq"), ("head", "sub"), None)
    in_specs = (tokens,) * 4 + (P(("head", "sub")), P(("groups", "seq"), ("head", "sub")))
    return jax.shard_map(
        functools.partial(per_device, mesh.shape["seq"]),
        mesh=mesh,
        in_specs=in_specs,
        out_specs=(tokens,) * 3,
        check_vma=False,
    )
```

```python
import functools

import jax
import jax.numpy as jnp
from jax import lax
from jax.experimental import pallas as pl
from jax.experimental.pallas import tpu as pltpu
from jax.sharding import PartitionSpec as P

VMEM = pl.BlockSpec(memory_space=pltpu.VMEM)
ANY = pl.BlockSpec(memory_space=pl.ANY)
BF16, F32 = jnp.bfloat16, jnp.float32
NT = (((1,), (1,)), ((), ()))
TN = (((0,), (0,)), ((), ()))
NN = (((1,), (0,)), ((), ()))
UNROLL = 4
CHUNKS = 3
DUE = {(0, 0): 5, (2, 1): 9}
MIB = 2**20
TOKEN = jax.ShapeDtypeStruct((8, 128), F32)


def dot(a, b, dims=NN):
    return lax.dot_general(a, b, dims, preferred_element_type=F32)


def running_forget(decay, spikes):
    heads, length = spikes.shape
    wide = -(-length // 128) * 128
    same = lax.broadcasted_iota(jnp.int32, (heads, heads), 0) == lax.broadcasted_iota(jnp.int32, (heads, heads), 1)
    exponent = jnp.sum(jnp.where(same, decay[...].astype(F32), 0.0), axis=1, keepdims=True)
    forget = jnp.exp2(-exponent) + spikes[...]
    if wide > length:
        forget = jnp.concatenate([forget, jnp.zeros((heads, wide - length), F32)], axis=1)
    lane = lax.broadcasted_iota(jnp.int32, forget.shape, 1)
    step = 1
    while step < length:
        forget = forget + jnp.where(lane >= step, pltpu.roll(forget, step, 1), 0.0)
        step *= 2
    return forget


def state_sum(left, right, fade):
    return dot((left.T.astype(F32) * fade).astype(BF16), right).astype(BF16)


def enter_of(within, h, length):
    return jnp.exp(-within[h : h + 1, :length])


def leave_of(within, h, length):
    return jnp.exp(within[h : h + 1, :length] - within[h : h + 1, length - 1 : length])


def first_kernel(count, heads, decay, spikes, q, k, v, g, *rest):
    payloads, (_, decay_v, spikes_v, left, right, sems) = rest[-6 - len(heads) : -6], rest[-6:]
    place = lax.axis_index("seq")
    length = spikes.shape[1]

    def run(a, b, fade_of):
        copies = [
            pltpu.make_async_copy(source, target, sems.at[i])
            for i, (source, target) in enumerate(
                ((spikes, spikes_v), (decay, decay_v), (a, left), (b, right))
            )
        ]
        for copy in copies:
            copy.start()
        for copy in copies[:2]:
            copy.wait()
        within = running_forget(decay_v, spikes_v)
        fades = {h: fade_of(within, h, length) for part in heads for h in part}
        for copy in copies[2:]:
            copy.wait()
        low = heads[0][0] // 8 * 8
        high = min(-(-(heads[-1][-1] + 1) // 8) * 8, left.shape[1])
        a_h = jnp.swapaxes(left[:, low:high, :], 0, 1)
        b_h = jnp.swapaxes(right[:, low:high, :], 0, 1)
        for part, payload in zip(heads, payloads):
            for i, h in enumerate(part):
                payload[i] = state_sum(a_h[h - low], b_h[h - low], fades[h])

    @pl.when(place == 0)
    def _():
        run(k, v, leave_of)

    @pl.when(place == count - 1)
    def _():
        run(q, g, enter_of)


def sums_kernel(count, decay, spikes, q, k, v, g, *rest):
    qh, kh, vh, gh, col, row, kv, grad, fade = rest[-9:]
    all_heads, length = spikes.shape
    place = lax.axis_index("seq")
    within = running_forget(decay, spikes)
    row[...] = within[:, None, :]
    fade[...] = jnp.broadcast_to(jnp.exp(-within[:, length - 1 : length])[:, :, None], fade.shape)
    kh[...] = jnp.swapaxes(k[...], 0, 1)
    vh[...] = jnp.swapaxes(v[...], 0, 1)
    qh[...] = jnp.swapaxes(q[...], 0, 1)
    gh[...] = jnp.swapaxes(g[...], 0, 1)

    @pl.when((place > 0) & (place < count - 1))
    def _():
        for h in range(all_heads):
            kv[h] = state_sum(kh[h], vh[h], leave_of(within, h, length))
            grad[h] = state_sum(qh[h], gh[h], enter_of(within, h, length))

    columns = within.T
    for h in range(all_heads):
        col[h] = jnp.broadcast_to(columns[:length, h : h + 1], (length, 128))


def merge_kernel(count, hop, start, got, kv, grad, fade, *rest):
    payload = rest[-2]
    place = lax.axis_index("seq")
    heads = got.shape[0]
    cut = slice(start, start + heads)
    for at, own in ((hop, kv), (count - 1 - hop, grad)):

        @pl.when(place == at)
        def _():
            payload[...] = (fade[cut] * got[...].astype(F32) + own[cut].astype(F32)).astype(BF16)


def intra_kernel(start, heads, col, row, qh, kh, vh, gh, *rest):
    qg, kg, vg = rest[-4:-1]
    length = qh.shape[1]
    edges = list(range(0, length, 256)) + [length]
    blocks = list(zip(edges[:-1], edges[1:]))

    def one(h, carry):
        q, k, v, g = qh[h], kh[h], vh[h], gh[h]
        qt, gt = q.T, g.T
        scores, probes = {}, {}
        for t0, t1 in blocks:
            for s0, s1 in blocks:
                if s0 > t0:
                    continue
                column = col[h, t0:t1, :]
                if s1 - s0 > 128:
                    column = jnp.concatenate([column, column], axis=1)
                spread = row[h, :, s0:s1] - column[:, : s1 - s0]
                weight = jnp.exp(jnp.minimum(spread, 0.0))
                if s0 == t0:
                    t = lax.broadcasted_iota(jnp.int32, spread.shape, 0)
                    s = lax.broadcasted_iota(jnp.int32, spread.shape, 1)
                    weight = jnp.where(t >= s, weight, 0.0)
                scores[t0, s0] = (dot(q[t0:t1], k[s0:s1], NT) * weight).astype(BF16)
                probes[t0, s0] = (dot(g[t0:t1], v[s0:s1], NT) * weight).astype(BF16)
        for t0, t1 in blocks:
            qg[h, t0:t1, :] = sum(dot(probes[t0, s0], k[s0:s1]) for s0, s1 in blocks if s0 <= t0)
        for s0, s1 in blocks:
            after = [(t0, t1) for t0, t1 in blocks if t0 >= s0]
            kg[h, s0:s1, :] = sum(dot(qt[:, t0:t1], probes[t0, s0]) for t0, t1 in after).T
            vg[h, s0:s1, :] = sum(dot(gt[:, t0:t1], scores[t0, s0]) for t0, t1 in after).T
        return carry

    lax.fori_loop(start, start + heads, one, 0, unroll=min(UNROLL, heads))


def terms(col, kh, vh, gh, state, start, h):
    length = kh.shape[1]

    def leave():
        return jnp.exp(col[h] - col[h, length - 1 : length, :])

    return (
        lambda: jnp.exp(-col[h]) * dot(gh[h], state[h - start], NT),
        lambda: leave() * dot(vh[h], state[h - start], NT),
        lambda: leave() * dot(kh[h], state[h - start]),
    )


def add_terms(which, target, slot, intra, col, kh, vh, gh, state, start, heads):
    def one(i, carry):
        h = start + i
        target[slot, i] = (intra[which][h] + terms(col, kh, vh, gh, state, start, h)[which]()).astype(BF16)
        return carry

    lax.fori_loop(0, heads, one, 0, unroll=min(2 * UNROLL, heads))


def out_copies(tokens, out, sem, parts=2):
    step = tokens.shape[0] // parts
    cuts = [slice(i * step, (i + 1) * step) for i in range(parts)]
    return [(cut, pltpu.make_async_copy(tokens.at[cut], out.at[cut], sem.at[i])) for i, cut in enumerate(cuts)]


def send_out(by_head, tokens, out, sem):
    for cut, copy in out_copies(tokens, out, sem):
        tokens[cut] = jnp.swapaxes(by_head[:, cut, :], 0, 1)
        copy.start()


def wait_out(tokens, out, sem):
    for _, copy in out_copies(tokens, out, sem):
        copy.wait()


def between_kernel(count, sizes, col, kh, vh, gh, qg, kg, vg, *rest):
    hops, chunks = count - 2, len(sizes)
    arrived = rest[: hops * chunks]
    *outs, state, by_head, tokens, sems = rest[-7:]
    intra = (qg, kg, vg)
    all_heads = kh.shape[0]
    place = lax.axis_index("seq")

    def take(end, came_from):
        @pl.when(place == end)
        def _():
            state[...] = jnp.zeros_like(state)

        for hop in range(1, count - 1):

            @pl.when(place == came_from(hop))
            def _():
                at = 0
                for c, heads in enumerate(sizes):
                    state[at : at + heads] = arrived[c * hops + hop - 1][...]
                    at += heads

    def write(which):
        add_terms(which, by_head, which, intra, col, kh, vh, gh, state, 0, all_heads)
        send_out(by_head[which], tokens.at[which], outs[which], sems.at[which])

    @pl.when(place < count - 1)
    def _():
        take(0, lambda hop: hop)
        write(0)

    @pl.when(place > 0)
    def _():
        take(count - 1, lambda hop: count - 1 - hop)
        write(1)
        write(2)

    @pl.when(place < count - 1)
    def _():
        wait_out(tokens.at[0], outs[0], sems.at[0])

    @pl.when(place > 0)
    def _():
        wait_out(tokens.at[1], outs[1], sems.at[1])
        wait_out(tokens.at[2], outs[2], sems.at[2])


def ends_kernel(count, start, col, kh, vh, gh, qg, kg, vg, got, *rest):
    by_head = rest[-1]
    heads = got.shape[0]
    place = lax.axis_index("seq")
    args = ((qg, kg, vg), col, kh, vh, gh, got, start, heads)

    @pl.when(place == count - 1)
    def _():
        add_terms(0, by_head, 0, *args)

    @pl.when(place == 0)
    def _():
        add_terms(1, by_head, 0, *args)
        add_terms(2, by_head, 1, *args)


def last_kernel(count, start, col, kh, vh, gh, qg, kg, vg, got, *rest):
    *outs, by_head, tokens, sems = rest[-6:]
    earlier = rest[:-9]
    heads = got.shape[0]
    place = lax.axis_index("seq")
    args = ((qg, kg, vg), col, kh, vh, gh, got, start, heads)

    def write(which, slot):
        add_terms(which, by_head, slot, *args)
        whole = jnp.concatenate([part[slot] for part in earlier] + [by_head[slot]], axis=0)
        send_out(whole, tokens.at[slot], outs[which], sems.at[slot])

    @pl.when(place == count - 1)
    def _():
        write(0, 0)
        wait_out(tokens.at[0], outs[0], sems.at[0])

    @pl.when(place == 0)
    def _():
        write(1, 0)
        write(2, 1)
        wait_out(tokens.at[0], outs[1], sems.at[0])
        wait_out(tokens.at[1], outs[2], sems.at[1])


def per_device(count, queries, keys, values, output_gradient, decay_exponent, forget_spikes):
    length, all_heads, size = queries.shape
    chunks = CHUNKS
    sizes = [all_heads // chunks + (c < all_heads % chunks) for c in range(chunks)]
    starts = [sum(sizes[:c]) for c in range(chunks)]
    spikes = forget_spikes.T
    shape = jax.ShapeDtypeStruct
    wide = -(-length // 128) * 128
    by_head = shape((all_heads, length, size), BF16)
    by_head_f = shape((all_heads, length, size), F32)
    states = shape((all_heads, size, size), BF16)
    full = shape(queries.shape, BF16)
    flops = 2 * length * size * size

    def state(c):
        return shape((sizes[c], size, size), BF16)

    def call(kernel, ins, outs, limit, cost, after=(), specs=None, out_spec=VMEM, **more):
        several = isinstance(outs, tuple)
        return pl.pallas_call(
            kernel,
            out_shape=outs,
            in_specs=(specs or [VMEM] * len(ins)) + [ANY] * len(after),
            out_specs=tuple(ANY if o is TOKEN else out_spec for o in outs) if several else out_spec,
            compiler_params=pltpu.CompilerParams(vmem_limit_bytes=limit * MIB),
            cost_estimate=pl.CostEstimate(flops=cost * flops, bytes_accessed=1 << 20, transcendentals=0),
            **more,
        )(*ins, *after)

    tensors = (queries, keys, values, output_gradient)
    raw = pltpu.VMEM(queries.shape, BF16)
    decay = decay_exponent[None, :]
    ranges = [range(a, a + n) for a, n in zip(starts, sizes)]
    payloads = []
    for part in (slice(0, 1), slice(1, chunks)):
        *several, token = call(
            functools.partial(first_kernel, count, ranges[part]),
            (decay, spikes, *tensors),
            (*(pltpu.VMEM((sizes[c], size, size), BF16) for c in range(chunks)[part]), TOKEN),
            52 if payloads else 60,
            sum(sizes[part]),
            specs=[ANY] * 6,
            scratch_shapes=[
                pltpu.VMEM(decay.shape, jnp.int32),
                pltpu.VMEM(spikes.shape, F32),
                raw,
                raw,
                pltpu.SemaphoreType.DMA((4,)),
            ],
        )
        payloads += several
    qh, kh, vh, gh, col, row, kv, grad, fade = call(
        functools.partial(sums_kernel, count),
        (decay, spikes, *tensors),
        (by_head,) * 4
        + (by_head_f, shape((all_heads, 1, wide), F32), states, states)
        + (shape((all_heads, 1, size), F32),),
        8,
        2 * all_heads,
        after=(token,),
    )

    intra, placed, done, merged = [], 0, (), ()
    ins = (col, row, qh, kh, vh, gh)

    def span_products(hop, chunk, before=None):
        nonlocal intra, placed, done
        due = all_heads if before is None else all_heads * DUE.get((hop, chunk), 0) // 16
        if due > placed:
            *intra, token = call(
                functools.partial(intra_kernel, placed, due - placed),
                (*ins, *intra),
                (by_head_f,) * 3 + (TOKEN,),
                8,
                5 * (due - placed),
                after=merged if before is None else before,
                input_output_aliases={len(ins) + j: j for j in range(len(intra))},
            )
            placed, done = due, (token,)

    arrived = [[] for _ in range(chunks)]
    span_products(0, 0, ())
    for hop in range(1, count):
        pairs = [(hop - 1, hop), (count - hop, count - hop - 1)]
        for c in range(chunks):
            got = lax.ppermute(payloads[c], "seq", pairs)
            arrived[c].append(got)
            if hop < count - 1:
                payloads[c], *merged = call(
                    functools.partial(merge_kernel, count, hop, starts[c]),
                    (got, kv, grad, fade),
                    (state(c), TOKEN),
                    4,
                    0,
                    after=done,
                )
                done = ()
                span_products(hop, c, merged)
    span_products(0, 0)

    common = (col, kh, vh, gh, *intra)
    came = [a for c in range(chunks) for a in arrived[c][:-1]]
    outs = call(
        functools.partial(between_kernel, count, sizes),
        (*common, *came),
        (full,) * 3,
        16,
        3 * all_heads,
        after=merged,
        out_spec=ANY,
        scratch_shapes=[
            pltpu.VMEM(states.shape, BF16),
            pltpu.VMEM((3,) + by_head.shape, BF16),
            pltpu.VMEM((3,) + full.shape, BF16),
            pltpu.SemaphoreType.DMA((3, 2)),
        ],
    )
    earlier = []
    for c in range(chunks - 1):
        earlier.append(
            call(
                functools.partial(ends_kernel, count, starts[c]),
                (*common, arrived[c][-1]),
                shape((2, sizes[c], length, size), BF16),
                8,
                2 * sizes[c],
                after=earlier[-1:],
            )
        )
    ins = (*common, arrived[-1][-1], *earlier)
    return tuple(
        call(
            functools.partial(last_kernel, count, starts[-1]),
            (*ins, *outs),
            (full,) * 3,
            8,
            2 * sizes[-1],
            specs=[VMEM] * len(ins) + [ANY] * 3,
            out_spec=ANY,
            scratch_shapes=[
                pltpu.VMEM((2, sizes[-1], length, size), BF16),
                pltpu.VMEM((2,) + full.shape, BF16),
                pltpu.SemaphoreType.DMA((2, 2)),
            ],
            input_output_aliases={len(ins) + j: j for j in range(3)},
        )
    )


def solution(mesh):
    tokens = P(("groups", "seq"), ("head", "sub"), None)
    in_specs = (tokens,) * 4 + (P(("head", "sub")), P(("groups", "seq"), ("head", "sub")))
    return jax.shard_map(
        functools.partial(per_device, mesh.shape["seq"]),
        mesh=mesh,
        in_specs=in_specs,
        out_specs=(tokens,) * 3,
        check_vma=False,
    )
```

```python
import functools

import jax
import jax.numpy as jnp
from jax import lax
from jax.experimental import pallas as pl
from jax.experimental.pallas import tpu as pltpu
from jax.sharding import PartitionSpec as P

VMEM = pl.BlockSpec(memory_space=pltpu.VMEM)
ANY = pl.BlockSpec(memory_space=pl.ANY)
BF16, F32 = jnp.bfloat16, jnp.float32
NT = (((1,), (1,)), ((), ()))
TN = (((0,), (0,)), ((), ()))
NN = (((1,), (0,)), ((), ()))
UNROLL = 4
CHUNKS = 3
DUE = {(0, 0): 5, (2, 1): 9}
MIB = 2**20
TOKEN = jax.ShapeDtypeStruct((8, 128), F32)


def dot(a, b, dims=NN):
    return lax.dot_general(a, b, dims, preferred_element_type=F32)


def running_forget(decay, spikes):
    heads, length = spikes.shape
    wide = -(-length // 128) * 128
    same = lax.broadcasted_iota(jnp.int32, (heads, heads), 0) == lax.broadcasted_iota(jnp.int32, (heads, heads), 1)
    exponent = jnp.sum(jnp.where(same, decay[...].astype(F32), 0.0), axis=1, keepdims=True)
    forget = jnp.exp2(-exponent) + spikes[...]
    if wide > length:
        forget = jnp.concatenate([forget, jnp.zeros((heads, wide - length), F32)], axis=1)
    lane = lax.broadcasted_iota(jnp.int32, forget.shape, 1)
    step = 1
    while step < length:
        forget = forget + jnp.where(lane >= step, pltpu.roll(forget, step, 1), 0.0)
        step *= 2
    return forget


def state_sum(left, right, fade):
    return dot((left.T.astype(F32) * fade).astype(BF16), right)


def enter_of(within, h, length):
    return jnp.exp(-within[h : h + 1, :length])


def leave_of(within, h, length):
    return jnp.exp(within[h : h + 1, :length] - within[h : h + 1, length - 1 : length])


def first_kernel(count, heads, decay, spikes, q, k, v, g, *rest):
    payloads, (_, decay_v, spikes_v, left, right, sems) = rest[-6 - len(heads) : -6], rest[-6:]
    place = lax.axis_index("seq")
    length = spikes.shape[1]

    middle = length * 3 // 4 // 128 * 128
    cuts = [slice(0, middle), slice(middle, length)] if middle else [slice(0, length)]
    low = heads[0][0] // 8 * 8
    high = min(-(-(heads[-1][-1] + 1) // 8) * 8, left.shape[1])
    mine = [h for part in heads for h in part]

    def run(a, b, fade_of):
        small = [
            pltpu.make_async_copy(spikes, spikes_v, sems.at[0]),
            pltpu.make_async_copy(decay, decay_v, sems.at[1]),
        ]
        pairs = [
            [
                pltpu.make_async_copy(a.at[cut], left.at[cut], sems.at[2 + 2 * i]),
                pltpu.make_async_copy(b.at[cut], right.at[cut], sems.at[3 + 2 * i]),
            ]
            for i, cut in enumerate(cuts)
        ]
        for copy in sum(pairs, small):
            copy.start()
        for copy in small:
            copy.wait()
        within = running_forget(decay_v, spikes_v)
        fades = {h: fade_of(within, h, length) for h in mine}
        sums = {h: 0.0 for h in mine}
        for cut, pair in zip(cuts, pairs):
            for copy in pair:
                copy.wait()
            a_h = jnp.swapaxes(left[cut, low:high, :], 0, 1)
            b_h = jnp.swapaxes(right[cut, low:high, :], 0, 1)
            for h in mine:
                sums[h] += state_sum(a_h[h - low], b_h[h - low], fades[h][:, cut])
        for part, payload in zip(heads, payloads):
            for i, h in enumerate(part):
                payload[i] = sums[h].astype(BF16)

    @pl.when(place == 0)
    def _():
        run(k, v, leave_of)

    @pl.when(place == count - 1)
    def _():
        run(q, g, enter_of)


def sums_kernel(count, decay, spikes, q, k, v, g, *rest):
    qh, kh, vh, gh, col, row, kv, grad, fade = rest[-9:]
    all_heads, length = spikes.shape
    place = lax.axis_index("seq")
    within = running_forget(decay, spikes)
    row[...] = within[:, None, :]
    fade[...] = jnp.broadcast_to(jnp.exp(-within[:, length - 1 : length])[:, :, None], fade.shape)
    kh[...] = jnp.swapaxes(k[...], 0, 1)
    vh[...] = jnp.swapaxes(v[...], 0, 1)
    qh[...] = jnp.swapaxes(q[...], 0, 1)
    gh[...] = jnp.swapaxes(g[...], 0, 1)

    @pl.when((place > 0) & (place < count - 1))
    def _():
        for h in range(all_heads):
            kv[h] = state_sum(kh[h], vh[h], leave_of(within, h, length)).astype(BF16)
            grad[h] = state_sum(qh[h], gh[h], enter_of(within, h, length)).astype(BF16)

    columns = within.T
    for h in range(all_heads):
        col[h] = jnp.broadcast_to(columns[:length, h : h + 1], (length, 128))


def merge_kernel(count, hop, start, got, kv, grad, fade, *rest):
    payload = rest[-2]
    place = lax.axis_index("seq")
    heads = got.shape[0]
    cut = slice(start, start + heads)
    for at, own in ((hop, kv), (count - 1 - hop, grad)):

        @pl.when(place == at)
        def _():
            payload[...] = (fade[cut] * got[...].astype(F32) + own[cut].astype(F32)).astype(BF16)


def intra_kernel(start, heads, col, row, qh, kh, vh, gh, *rest):
    qg, kg, vg = rest[-4:-1]
    length = qh.shape[1]
    edges = list(range(0, length, 256)) + [length]
    blocks = list(zip(edges[:-1], edges[1:]))

    def one(h, carry):
        q, k, v, g = qh[h], kh[h], vh[h], gh[h]
        qt, gt = q.T, g.T
        scores, probes = {}, {}
        for t0, t1 in blocks:
            for s0, s1 in blocks:
                if s0 > t0:
                    continue
                column = col[h, t0:t1, :]
                if s1 - s0 > 128:
                    column = jnp.concatenate([column, column], axis=1)
                spread = row[h, :, s0:s1] - column[:, : s1 - s0]
                weight = jnp.exp(jnp.minimum(spread, 0.0))
                if s0 == t0:
                    t = lax.broadcasted_iota(jnp.int32, spread.shape, 0)
                    s = lax.broadcasted_iota(jnp.int32, spread.shape, 1)
                    weight = jnp.where(t >= s, weight, 0.0)
                scores[t0, s0] = (dot(q[t0:t1], k[s0:s1], NT) * weight).astype(BF16)
                probes[t0, s0] = (dot(g[t0:t1], v[s0:s1], NT) * weight).astype(BF16)
        for t0, t1 in blocks:
            qg[h, t0:t1, :] = sum(dot(probes[t0, s0], k[s0:s1]) for s0, s1 in blocks if s0 <= t0)
        for s0, s1 in blocks:
            after = [(t0, t1) for t0, t1 in blocks if t0 >= s0]
            kg[h, s0:s1, :] = sum(dot(qt[:, t0:t1], probes[t0, s0]) for t0, t1 in after).T
            vg[h, s0:s1, :] = sum(dot(gt[:, t0:t1], scores[t0, s0]) for t0, t1 in after).T
        return carry

    lax.fori_loop(start, start + heads, one, 0, unroll=min(2 * UNROLL, heads))


def terms(col, kh, vh, gh, state, start, h):
    length = kh.shape[1]

    def leave():
        return jnp.exp(col[h] - col[h, length - 1 : length, :])

    return (
        lambda: jnp.exp(-col[h]) * dot(gh[h], state[h - start], NT),
        lambda: leave() * dot(vh[h], state[h - start], NT),
        lambda: leave() * dot(kh[h], state[h - start]),
    )


def add_terms(which, target, slot, intra, col, kh, vh, gh, state, start, heads):
    def one(i, carry):
        h = start + i
        target[slot, i] = (intra[which][h] + terms(col, kh, vh, gh, state, start, h)[which]()).astype(BF16)
        return carry

    lax.fori_loop(0, heads, one, 0, unroll=min(2 * UNROLL, heads))


def out_copies(tokens, out, sem, parts=2):
    step = tokens.shape[0] // parts
    cuts = [slice(i * step, (i + 1) * step) for i in range(parts)]
    return [(cut, pltpu.make_async_copy(tokens.at[cut], out.at[cut], sem.at[i])) for i, cut in enumerate(cuts)]


def send_out(by_head, tokens, out, sem):
    for cut, copy in out_copies(tokens, out, sem):
        tokens[cut] = jnp.swapaxes(by_head[:, cut, :], 0, 1)
        copy.start()


def wait_out(tokens, out, sem):
    for _, copy in out_copies(tokens, out, sem):
        copy.wait()


def between_kernel(count, sizes, col, kh, vh, gh, qg, kg, vg, *rest):
    hops, chunks = count - 2, len(sizes)
    arrived = rest[: hops * chunks]
    *outs, state, by_head, tokens, sems = rest[-7:]
    intra = (qg, kg, vg)
    all_heads = kh.shape[0]
    place = lax.axis_index("seq")

    def take(end, came_from):
        @pl.when(place == end)
        def _():
            state[...] = jnp.zeros_like(state)

        for hop in range(1, count - 1):

            @pl.when(place == came_from(hop))
            def _():
                at = 0
                for c, heads in enumerate(sizes):
                    state[at : at + heads] = arrived[c * hops + hop - 1][...]
                    at += heads

    def write(which):
        add_terms(which, by_head, which, intra, col, kh, vh, gh, state, 0, all_heads)
        send_out(by_head[which], tokens.at[which], outs[which], sems.at[which])

    @pl.when(place < count - 1)
    def _():
        take(0, lambda hop: hop)
        write(0)

    @pl.when(place > 0)
    def _():
        take(count - 1, lambda hop: count - 1 - hop)
        write(1)
        write(2)

    @pl.when(place < count - 1)
    def _():
        wait_out(tokens.at[0], outs[0], sems.at[0])

    @pl.when(place > 0)
    def _():
        wait_out(tokens.at[1], outs[1], sems.at[1])
        wait_out(tokens.at[2], outs[2], sems.at[2])


def some_heads(parts, starts, low, high, slot):
    pieces = []
    for part, start in zip(parts, starts):
        first, last = max(low - start, 0), min(high - start, part.shape[1])
        if first < last:
            pieces.append(part[slot, first:last])
    return jnp.concatenate(pieces, axis=0)


def ends_kernel(count, starts, c, ready, col, kh, vh, gh, qg, kg, vg, got, *rest):
    by_head, tokens = rest[-2:] if ready else (rest[-1], None)
    parts = [*rest[:c], by_head]
    heads = got.shape[0]
    place = lax.axis_index("seq")
    args = ((qg, kg, vg), col, kh, vh, gh, got, starts[c], heads)

    def lay_out(slot):
        if ready:
            tokens[slot, :, :ready, :] = jnp.swapaxes(some_heads(parts, starts, 0, ready, slot), 0, 1)

    @pl.when(place == count - 1)
    def _():
        add_terms(0, by_head, 0, *args)
        lay_out(0)

    @pl.when(place == 0)
    def _():
        add_terms(1, by_head, 0, *args)
        add_terms(2, by_head, 1, *args)
        lay_out(0)
        lay_out(1)


def last_kernel(count, starts, ready, col, kh, vh, gh, qg, kg, vg, got, *rest):
    *outs, tokens, by_head, sems = rest[-6:]
    parts = [*rest[: len(starts) - 1], by_head]
    all_heads = kh.shape[0]
    place = lax.axis_index("seq")
    args = ((qg, kg, vg), col, kh, vh, gh, got, starts[-1], got.shape[0])

    def write(which, slot):
        add_terms(which, by_head, slot, *args)
        whole = some_heads(parts, starts, ready, all_heads, slot)
        for cut, copy in out_copies(tokens.at[slot], outs[which], sems.at[slot]):
            tokens[slot, cut, ready:, :] = jnp.swapaxes(whole[:, cut, :], 0, 1)
            copy.start()

    @pl.when(place == count - 1)
    def _():
        write(0, 0)
        wait_out(tokens.at[0], outs[0], sems.at[0])

    @pl.when(place == 0)
    def _():
        write(1, 0)
        write(2, 1)
        wait_out(tokens.at[0], outs[1], sems.at[0])
        wait_out(tokens.at[1], outs[2], sems.at[1])


def per_device(count, queries, keys, values, output_gradient, decay_exponent, forget_spikes):
    length, all_heads, size = queries.shape
    chunks = CHUNKS
    sizes = [all_heads // chunks + (c < all_heads % chunks) for c in range(chunks)]
    starts = [sum(sizes[:c]) for c in range(chunks)]
    spikes = forget_spikes.T
    shape = jax.ShapeDtypeStruct
    wide = -(-length // 128) * 128
    by_head = shape((all_heads, length, size), BF16)
    by_head_f = shape((all_heads, length, size), F32)
    states = shape((all_heads, size, size), BF16)
    full = shape(queries.shape, BF16)
    flops = 2 * length * size * size

    def state(c):
        return shape((sizes[c], size, size), BF16)

    def call(kernel, ins, outs, limit, cost, after=(), specs=None, out_spec=VMEM, **more):
        several = isinstance(outs, tuple)
        return pl.pallas_call(
            kernel,
            out_shape=outs,
            in_specs=(specs or [VMEM] * len(ins)) + [ANY] * len(after),
            out_specs=tuple(ANY if o is TOKEN else out_spec for o in outs) if several else out_spec,
            compiler_params=pltpu.CompilerParams(vmem_limit_bytes=limit * MIB),
            cost_estimate=pl.CostEstimate(flops=cost * flops, bytes_accessed=1 << 20, transcendentals=0),
            **more,
        )(*ins, *after)

    tensors = (queries, keys, values, output_gradient)
    raw = pltpu.VMEM(queries.shape, BF16)
    decay = decay_exponent[None, :]
    ranges = [range(a, a + n) for a, n in zip(starts, sizes)]
    payloads = []
    for part in (slice(0, 1), slice(1, chunks)):
        *several, token = call(
            functools.partial(first_kernel, count, ranges[part]),
            (decay, spikes, *tensors),
            (*(pltpu.VMEM((sizes[c], size, size), BF16) for c in range(chunks)[part]), TOKEN),
            52 if payloads else 60,
            sum(sizes[part]),
            specs=[ANY] * 6,
            scratch_shapes=[
                pltpu.VMEM(decay.shape, jnp.int32),
                pltpu.VMEM(spikes.shape, F32),
                raw,
                raw,
                pltpu.SemaphoreType.DMA((6,)),
            ],
        )
        payloads += several
    qh, kh, vh, gh, col, row, kv, grad, fade = call(
        functools.partial(sums_kernel, count),
        (decay, spikes, *tensors),
        (by_head,) * 4
        + (by_head_f, shape((all_heads, 1, wide), F32), states, states)
        + (shape((all_heads, 1, size), F32),),
        8,
        2 * all_heads,
        after=(token,),
    )

    intra, placed, done, merged = [], 0, (), ()
    ins = (col, row, qh, kh, vh, gh)

    def span_products(hop, chunk, before=None):
        nonlocal intra, placed, done
        due = all_heads if before is None else all_heads * DUE.get((hop, chunk), 0) // 16
        if due > placed:
            *intra, token = call(
                functools.partial(intra_kernel, placed, due - placed),
                (*ins, *intra),
                (by_head_f,) * 3 + (TOKEN,),
                8,
                5 * (due - placed),
                after=merged if before is None else before,
                input_output_aliases={len(ins) + j: j for j in range(len(intra))},
            )
            placed, done = due, (token,)

    arrived = [[] for _ in range(chunks)]
    span_products(0, 0, ())
    for hop in range(1, count):
        pairs = [(hop - 1, hop), (count - hop, count - hop - 1)]
        for c in range(chunks):
            got = lax.ppermute(payloads[c], "seq", pairs)
            arrived[c].append(got)
            if hop < count - 1:
                payloads[c], *merged = call(
                    functools.partial(merge_kernel, count, hop, starts[c]),
                    (got, kv, grad, fade),
                    (state(c), TOKEN),
                    4,
                    0,
                    after=done,
                )
                done = ()
                span_products(hop, c, merged)
    span_products(0, 0)

    common = (col, kh, vh, gh, *intra)
    came = [a for c in range(chunks) for a in arrived[c][:-1]]
    outs = call(
        functools.partial(between_kernel, count, sizes),
        (*common, *came),
        (full,) * 3,
        16,
        3 * all_heads,
        after=merged,
        out_spec=ANY,
        scratch_shapes=[
            pltpu.VMEM(states.shape, BF16),
            pltpu.VMEM((3,) + by_head.shape, BF16),
            pltpu.VMEM((3,) + full.shape, BF16),
            pltpu.SemaphoreType.DMA((3, 2)),
        ],
    )
    ready = starts[-1] // 8 * 8
    laid = shape((2,) + full.shape, BF16)
    earlier, tokens = [], ()
    for c in range(chunks - 1):
        lays = ready if c == chunks - 2 else 0
        part, *tokens = call(
            functools.partial(ends_kernel, count, starts, c, lays),
            (*common, arrived[c][-1], *earlier),
            (shape((2, sizes[c], length, size), BF16),) + ((laid,) if lays else ()),
            16,
            2 * sizes[c],
        )
        earlier.append(part)
    ins = (*common, arrived[-1][-1], *earlier, *tokens, *outs)
    fixed = len(ins) - 3
    aliases = {fixed + j: j for j in range(3)}
    if tokens:
        aliases[fixed - 1] = 3
    vmem, any_space = [VMEM] * fixed, [ANY] * 3
    *outs, _ = pl.pallas_call(
        functools.partial(last_kernel, count, starts, ready),
        out_shape=(full,) * 3 + (laid,),
        in_specs=vmem + any_space,
        out_specs=(ANY,) * 3 + (VMEM,),
        scratch_shapes=[
            pltpu.VMEM((2, sizes[-1], length, size), BF16),
            pltpu.SemaphoreType.DMA((2, 2)),
        ],
        compiler_params=pltpu.CompilerParams(vmem_limit_bytes=8 * MIB),
        cost_estimate=pl.CostEstimate(flops=2 * sizes[-1] * flops, bytes_accessed=1 << 20, transcendentals=0),
        input_output_aliases=aliases,
    )(*ins)
    return tuple(outs)


def solution(mesh):
    tokens = P(("groups", "seq"), ("head", "sub"), None)
    in_specs = (tokens,) * 4 + (P(("head", "sub")), P(("groups", "seq"), ("head", "sub")))
    return jax.shard_map(
        functools.partial(per_device, mesh.shape["seq"]),
        mesh=mesh,
        in_specs=in_specs,
        out_specs=(tokens,) * 3,
        check_vma=False,
    )
```

```python
import functools

import jax
import jax.numpy as jnp
from jax import lax
from jax.experimental import pallas as pl
from jax.experimental.pallas import tpu as pltpu
from jax.sharding import PartitionSpec as P

VMEM = pl.BlockSpec(memory_space=pltpu.VMEM)
ANY = pl.BlockSpec(memory_space=pl.ANY)
BF16, F32 = jnp.bfloat16, jnp.float32
NT = (((1,), (1,)), ((), ()))
TN = (((0,), (0,)), ((), ()))
NN = (((1,), (0,)), ((), ()))
UNROLL = 4
CHUNKS = 3
FIRST_LIMIT, SUMS_LIMIT = 63, 49
DUE = {(0, 0): 2, (2, 1): 6}
MIB = 2**20
TOKEN = jax.ShapeDtypeStruct((8, 128), F32)


def dot(a, b, dims=NN):
    return lax.dot_general(a, b, dims, preferred_element_type=F32)


def running_forget(decay, spikes):
    heads, length = spikes.shape
    wide = -(-length // 128) * 128
    same = lax.broadcasted_iota(jnp.int32, (heads, heads), 0) == lax.broadcasted_iota(jnp.int32, (heads, heads), 1)
    exponent = jnp.sum(jnp.where(same, decay[...].astype(F32), 0.0), axis=1, keepdims=True)
    forget = jnp.exp2(-exponent) + spikes[...]
    if wide > length:
        forget = jnp.concatenate([forget, jnp.zeros((heads, wide - length), F32)], axis=1)
    lane = lax.broadcasted_iota(jnp.int32, forget.shape, 1)
    step = 1
    while step < length:
        forget = forget + jnp.where(lane >= step, pltpu.roll(forget, step, 1), 0.0)
        step *= 2
    return forget


def state_sum(left, right, fade):
    return dot((left.T.astype(F32) * fade).astype(BF16), right)


def enter_of(within, h, length):
    return jnp.exp(-within[h : h + 1, :length])


def leave_of(within, h, length):
    return jnp.exp(within[h : h + 1, :length] - within[h : h + 1, length - 1 : length])


def first_kernel(count, heads, decay, spikes, q, k, v, g, *rest):
    payloads, (_, decay_v, spikes_v, left, right, sems) = rest[-6 - len(heads) : -6], rest[-6:]
    place = lax.axis_index("seq")
    length = spikes.shape[1]

    middle = length * 3 // 4 // 128 * 128
    cuts = [slice(0, middle), slice(middle, length)] if middle else [slice(0, length)]
    low = heads[0][0] // 8 * 8
    high = min(-(-(heads[-1][-1] + 1) // 8) * 8, left.shape[1])
    mine = [h for part in heads for h in part]

    def run(a, b, fade_of):
        small = [
            pltpu.make_async_copy(spikes, spikes_v, sems.at[0]),
            pltpu.make_async_copy(decay, decay_v, sems.at[1]),
        ]
        pairs = [
            [
                pltpu.make_async_copy(a.at[cut], left.at[cut], sems.at[2 + 2 * i]),
                pltpu.make_async_copy(b.at[cut], right.at[cut], sems.at[3 + 2 * i]),
            ]
            for i, cut in enumerate(cuts)
        ]
        for copy in sum(pairs, small):
            copy.start()
        for copy in small:
            copy.wait()
        within = running_forget(decay_v, spikes_v)
        fades = {h: fade_of(within, h, length) for h in mine}
        sums = {h: 0.0 for h in mine}
        for cut, pair in zip(cuts, pairs):
            for copy in pair:
                copy.wait()
            a_h = jnp.swapaxes(left[cut, low:high, :], 0, 1)
            b_h = jnp.swapaxes(right[cut, low:high, :], 0, 1)
            for h in mine:
                sums[h] += state_sum(a_h[h - low], b_h[h - low], fades[h][:, cut])
        for part, payload in zip(heads, payloads):
            for i, h in enumerate(part):
                payload[i] = sums[h].astype(BF16)

    @pl.when(place == 0)
    def _():
        run(k, v, leave_of)

    @pl.when(place == count - 1)
    def _():
        run(q, g, enter_of)


def sums_kernel(count, decay, spikes, q, k, v, g, *rest):
    qh, kh, vh, gh, col, row, kv, grad, fade = rest[-16:-7]
    decay_v, spikes_v, *raws, sems = rest[-7:]
    all_heads, length = spikes.shape
    place = lax.axis_index("seq")
    moves = ((spikes, spikes_v), (decay, decay_v), *zip((k, v, q, g), raws))
    copies = [pltpu.make_async_copy(source, target, sems.at[i]) for i, (source, target) in enumerate(moves)]
    for copy in copies:
        copy.start()
    for copy in copies[:2]:
        copy.wait()
    within = running_forget(decay_v, spikes_v)
    row[...] = within[:, None, :]
    fade[...] = jnp.broadcast_to(jnp.exp(-within[:, length - 1 : length])[:, :, None], fade.shape)
    columns = within.T
    for h in range(all_heads):
        col[h] = jnp.broadcast_to(columns[:length, h : h + 1], (length, 128))
    for copy, raw, target in zip(copies[2:], raws, (kh, vh, qh, gh)):
        copy.wait()
        target[...] = jnp.swapaxes(raw[...], 0, 1)

    @pl.when((place > 0) & (place < count - 1))
    def _():
        for h in range(all_heads):
            kv[h] = state_sum(kh[h], vh[h], leave_of(within, h, length)).astype(BF16)
            grad[h] = state_sum(qh[h], gh[h], enter_of(within, h, length)).astype(BF16)


def merge_kernel(count, hop, start, got, kv, grad, fade, *rest):
    payload = rest[-2]
    place = lax.axis_index("seq")
    heads = got.shape[0]
    cut = slice(start, start + heads)
    for at, own in ((hop, kv), (count - 1 - hop, grad)):

        @pl.when(place == at)
        def _():
            payload[...] = (fade[cut] * got[...].astype(F32) + own[cut].astype(F32)).astype(BF16)


def intra_kernel(start, heads, col, row, qh, kh, vh, gh, *rest):
    qg, kg, vg = rest[-4:-1]
    length = qh.shape[1]
    edges = list(range(0, length, 256)) + [length]
    blocks = list(zip(edges[:-1], edges[1:]))

    def one(h, carry):
        q, k, v, g = qh[h], kh[h], vh[h], gh[h]
        qt, gt = q.T, g.T
        scores, probes = {}, {}
        for t0, t1 in blocks:
            for s0, s1 in blocks:
                if s0 > t0:
                    continue
                column = col[h, t0:t1, :]
                if s1 - s0 > 128:
                    column = jnp.concatenate([column, column], axis=1)
                spread = row[h, :, s0:s1] - column[:, : s1 - s0]
                weight = jnp.exp(jnp.minimum(spread, 0.0))
                if s0 == t0:
                    t = lax.broadcasted_iota(jnp.int32, spread.shape, 0)
                    s = lax.broadcasted_iota(jnp.int32, spread.shape, 1)
                    weight = jnp.where(t >= s, weight, 0.0)
                scores[t0, s0] = (dot(q[t0:t1], k[s0:s1], NT) * weight).astype(BF16)
                probes[t0, s0] = (dot(g[t0:t1], v[s0:s1], NT) * weight).astype(BF16)
        for t0, t1 in blocks:
            qg[h, t0:t1, :] = sum(dot(probes[t0, s0], k[s0:s1]) for s0, s1 in blocks if s0 <= t0)
        for s0, s1 in blocks:
            after = [(t0, t1) for t0, t1 in blocks if t0 >= s0]
            kg[h, s0:s1, :] = sum(dot(qt[:, t0:t1], probes[t0, s0]) for t0, t1 in after).T
            vg[h, s0:s1, :] = sum(dot(gt[:, t0:t1], scores[t0, s0]) for t0, t1 in after).T
        return carry

    lax.fori_loop(start, start + heads, one, 0, unroll=min(2 * UNROLL, heads))


def terms(col, kh, vh, gh, state, start, h):
    length = kh.shape[1]

    def leave():
        return jnp.exp(col[h] - col[h, length - 1 : length, :])

    return (
        lambda: jnp.exp(-col[h]) * dot(gh[h], state[h - start], NT),
        lambda: leave() * dot(vh[h], state[h - start], NT),
        lambda: leave() * dot(kh[h], state[h - start]),
    )


def add_terms(which, target, slot, intra, col, kh, vh, gh, state, start, heads):
    def one(i, carry):
        h = start + i
        target[slot, i] = (intra[which][h] + terms(col, kh, vh, gh, state, start, h)[which]()).astype(BF16)
        return carry

    lax.fori_loop(0, heads, one, 0, unroll=min(2 * UNROLL, heads))


def out_copies(tokens, out, sem, parts=2):
    step = tokens.shape[0] // parts
    cuts = [slice(i * step, (i + 1) * step) for i in range(parts)]
    return [(cut, pltpu.make_async_copy(tokens.at[cut], out.at[cut], sem.at[i])) for i, cut in enumerate(cuts)]


def send_out(by_head, tokens, out, sem):
    for cut, copy in out_copies(tokens, out, sem):
        tokens[cut] = jnp.swapaxes(by_head[:, cut, :], 0, 1)
        copy.start()


def wait_out(tokens, out, sem):
    for _, copy in out_copies(tokens, out, sem):
        copy.wait()


def between_kernel(count, sizes, col, kh, vh, gh, qg, kg, vg, *rest):
    hops, chunks = count - 2, len(sizes)
    arrived = rest[: hops * chunks]
    *outs, state, by_head, tokens, sems = rest[-7:]
    intra = (qg, kg, vg)
    all_heads = kh.shape[0]
    place = lax.axis_index("seq")

    def take(end, came_from):
        @pl.when(place == end)
        def _():
            state[...] = jnp.zeros_like(state)

        for hop in range(1, count - 1):

            @pl.when(place == came_from(hop))
            def _():
                at = 0
                for c, heads in enumerate(sizes):
                    state[at : at + heads] = arrived[c * hops + hop - 1][...]
                    at += heads

    def write(which):
        add_terms(which, by_head, which, intra, col, kh, vh, gh, state, 0, all_heads)
        send_out(by_head[which], tokens.at[which], outs[which], sems.at[which])

    @pl.when(place < count - 1)
    def _():
        take(0, lambda hop: hop)
        write(0)

    @pl.when(place > 0)
    def _():
        take(count - 1, lambda hop: count - 1 - hop)
        write(1)
        write(2)

    @pl.when(place < count - 1)
    def _():
        wait_out(tokens.at[0], outs[0], sems.at[0])

    @pl.when(place > 0)
    def _():
        wait_out(tokens.at[1], outs[1], sems.at[1])
        wait_out(tokens.at[2], outs[2], sems.at[2])


def some_heads(parts, starts, low, high, slot):
    pieces = []
    for part, start in zip(parts, starts):
        first, last = max(low - start, 0), min(high - start, part.shape[1])
        if first < last:
            pieces.append(part[slot, first:last])
    return jnp.concatenate(pieces, axis=0)


def ends_kernel(count, starts, c, ready, col, kh, vh, gh, qg, kg, vg, got, *rest):
    by_head, tokens = rest[-2:] if ready else (rest[-1], None)
    parts = [*rest[:c], by_head]
    heads = got.shape[0]
    place = lax.axis_index("seq")
    args = ((qg, kg, vg), col, kh, vh, gh, got, starts[c], heads)

    def lay_out(slot):
        if ready:
            tokens[slot, :, :ready, :] = jnp.swapaxes(some_heads(parts, starts, 0, ready, slot), 0, 1)

    @pl.when(place == count - 1)
    def _():
        add_terms(0, by_head, 0, *args)
        lay_out(0)

    @pl.when(place == 0)
    def _():
        add_terms(1, by_head, 0, *args)
        add_terms(2, by_head, 1, *args)
        lay_out(0)
        lay_out(1)


def last_kernel(count, starts, ready, col, kh, vh, gh, qg, kg, vg, got, *rest):
    *outs, tokens, by_head, sems = rest[-6:]
    parts = [*rest[: len(starts) - 1], by_head]
    all_heads = kh.shape[0]
    place = lax.axis_index("seq")
    args = ((qg, kg, vg), col, kh, vh, gh, got, starts[-1], got.shape[0])

    def write(which, slot):
        add_terms(which, by_head, slot, *args)
        whole = some_heads(parts, starts, ready, all_heads, slot)
        for cut, copy in out_copies(tokens.at[slot], outs[which], sems.at[slot]):
            tokens[slot, cut, ready:, :] = jnp.swapaxes(whole[:, cut, :], 0, 1)
            copy.start()

    @pl.when(place == count - 1)
    def _():
        write(0, 0)
        wait_out(tokens.at[0], outs[0], sems.at[0])

    @pl.when(place == 0)
    def _():
        write(1, 0)
        write(2, 1)
        wait_out(tokens.at[0], outs[1], sems.at[0])
        wait_out(tokens.at[1], outs[2], sems.at[1])


def per_device(count, queries, keys, values, output_gradient, decay_exponent, forget_spikes):
    length, all_heads, size = queries.shape
    chunks = CHUNKS
    sizes = [all_heads // chunks + (c < all_heads % chunks) for c in range(chunks)]
    starts = [sum(sizes[:c]) for c in range(chunks)]
    spikes = forget_spikes.T
    shape = jax.ShapeDtypeStruct
    wide = -(-length // 128) * 128
    by_head = shape((all_heads, length, size), BF16)
    by_head_f = shape((all_heads, length, size), F32)
    states = shape((all_heads, size, size), BF16)
    full = shape(queries.shape, BF16)
    flops = 2 * length * size * size

    def state(c):
        return shape((sizes[c], size, size), BF16)

    def call(kernel, ins, outs, limit, cost, after=(), specs=None, out_spec=VMEM, **more):
        several = isinstance(outs, tuple)
        return pl.pallas_call(
            kernel,
            out_shape=outs,
            in_specs=(specs or [VMEM] * len(ins)) + [ANY] * len(after),
            out_specs=tuple(ANY if o is TOKEN else out_spec for o in outs) if several else out_spec,
            compiler_params=pltpu.CompilerParams(vmem_limit_bytes=limit * MIB),
            cost_estimate=pl.CostEstimate(flops=cost * flops, bytes_accessed=1 << 20, transcendentals=0),
            **more,
        )(*ins, *after)

    tensors = (queries, keys, values, output_gradient)
    raw = pltpu.VMEM(queries.shape, BF16)
    decay = decay_exponent[None, :]
    ranges = [range(a, a + n) for a, n in zip(starts, sizes)]
    payloads = []
    for part in (slice(0, 1), slice(1, chunks)):
        *several, token = call(
            functools.partial(first_kernel, count, ranges[part]),
            (decay, spikes, *tensors),
            (*(pltpu.VMEM((sizes[c], size, size), BF16) for c in range(chunks)[part]), TOKEN),
            FIRST_LIMIT,
            sum(sizes[part]),
            specs=[ANY] * 6,
            scratch_shapes=[
                pltpu.VMEM(decay.shape, jnp.int32),
                pltpu.VMEM(spikes.shape, F32),
                raw,
                raw,
                pltpu.SemaphoreType.DMA((6,)),
            ],
        )
        payloads += several
    qh, kh, vh, gh, col, row, kv, grad, fade = call(
        functools.partial(sums_kernel, count),
        (decay, spikes, *tensors),
        tuple(
            pltpu.VMEM(o.shape, o.dtype)
            for o in (*(by_head,) * 4, by_head_f, shape((all_heads, 1, wide), F32))
            + (states, states, shape((all_heads, 1, size), F32))
        ),
        SUMS_LIMIT,
        2 * all_heads,
        after=payloads[-1:],
        specs=[ANY] * 6,
        scratch_shapes=[
            pltpu.VMEM(decay.shape, jnp.int32),
            pltpu.VMEM(spikes.shape, F32),
            raw,
            raw,
            raw,
            raw,
            pltpu.SemaphoreType.DMA((6,)),
        ],
    )

    intra, placed, done, merged = [], 0, (), ()
    ins = (col, row, qh, kh, vh, gh)

    def span_products(hop, chunk, before=None):
        nonlocal intra, placed, done
        due = all_heads if before is None else all_heads * DUE.get((hop, chunk), 0) // 16
        if due > placed:
            *intra, token = call(
                functools.partial(intra_kernel, placed, due - placed),
                (*ins, *intra),
                (by_head_f,) * 3 + (TOKEN,),
                8,
                5 * (due - placed),
                after=merged if before is None else before,
                input_output_aliases={len(ins) + j: j for j in range(len(intra))},
            )
            placed, done = due, (token,)

    arrived = [[] for _ in range(chunks)]
    span_products(0, 0, ())
    for hop in range(1, count):
        pairs = [(hop - 1, hop), (count - hop, count - hop - 1)]
        for c in range(chunks):
            got = lax.ppermute(payloads[c], "seq", pairs)
            arrived[c].append(got)
            if hop < count - 1:
                payloads[c], *merged = call(
                    functools.partial(merge_kernel, count, hop, starts[c]),
                    (got, kv, grad, fade),
                    (state(c), TOKEN),
                    4,
                    0,
                    after=done,
                )
                done = ()
                span_products(hop, c, merged)
    span_products(0, 0)

    common = (col, kh, vh, gh, *intra)
    came = [a for c in range(chunks) for a in arrived[c][:-1]]
    outs = call(
        functools.partial(between_kernel, count, sizes),
        (*common, *came),
        (full,) * 3,
        16,
        3 * all_heads,
        after=merged,
        out_spec=ANY,
        scratch_shapes=[
            pltpu.VMEM(states.shape, BF16),
            pltpu.VMEM((3,) + by_head.shape, BF16),
            pltpu.VMEM((3,) + full.shape, BF16),
            pltpu.SemaphoreType.DMA((3, 2)),
        ],
    )
    ready = starts[-1] // 8 * 8
    laid = shape((2,) + full.shape, BF16)
    earlier, tokens = [], ()
    for c in range(chunks - 1):
        lays = ready if c == chunks - 2 else 0
        part, *tokens = call(
            functools.partial(ends_kernel, count, starts, c, lays),
            (*common, arrived[c][-1], *earlier),
            (shape((2, sizes[c], length, size), BF16),) + ((laid,) if lays else ()),
            16,
            2 * sizes[c],
        )
        earlier.append(part)
    ins = (*common, arrived[-1][-1], *earlier, *tokens, *outs)
    fixed = len(ins) - 3
    aliases = {fixed + j: j for j in range(3)}
    if tokens:
        aliases[fixed - 1] = 3
    vmem, any_space = [VMEM] * fixed, [ANY] * 3
    *outs, _ = pl.pallas_call(
        functools.partial(last_kernel, count, starts, ready),
        out_shape=(full,) * 3 + (laid,),
        in_specs=vmem + any_space,
        out_specs=(ANY,) * 3 + (VMEM,),
        scratch_shapes=[
            pltpu.VMEM((2, sizes[-1], length, size), BF16),
            pltpu.SemaphoreType.DMA((2, 2)),
        ],
        compiler_params=pltpu.CompilerParams(vmem_limit_bytes=8 * MIB),
        cost_estimate=pl.CostEstimate(flops=2 * sizes[-1] * flops, bytes_accessed=1 << 20, transcendentals=0),
        input_output_aliases=aliases,
    )(*ins)
    return tuple(outs)


def solution(mesh):
    tokens = P(("groups", "seq"), ("head", "sub"), None)
    in_specs = (tokens,) * 4 + (P(("head", "sub")), P(("groups", "seq"), ("head", "sub")))
    return jax.shard_map(
        functools.partial(per_device, mesh.shape["seq"]),
        mesh=mesh,
        in_specs=in_specs,
        out_specs=(tokens,) * 3,
        check_vma=False,
    )
```

```python
import functools

import jax
import jax.numpy as jnp
from jax import lax
from jax.experimental import pallas as pl
from jax.experimental.pallas import tpu as pltpu
from jax.sharding import PartitionSpec as P

VMEM = pl.BlockSpec(memory_space=pltpu.VMEM)
ANY = pl.BlockSpec(memory_space=pl.ANY)
BF16, F32 = jnp.bfloat16, jnp.float32
NT = (((1,), (1,)), ((), ()))
TN = (((0,), (0,)), ((), ()))
NN = (((1,), (0,)), ((), ()))
UNROLL = 4
CHUNKS = 3
FIRST_LIMIT, SUMS_LIMIT = 63, 49
DUE = {(0, 0): 1, (2, 1): 6}
MIB = 2**20
TOKEN = jax.ShapeDtypeStruct((8, 128), F32)


def dot(a, b, dims=NN):
    return lax.dot_general(a, b, dims, preferred_element_type=F32)


def running_forget(decay, spikes):
    heads, length = spikes.shape
    wide = -(-length // 128) * 128
    same = lax.broadcasted_iota(jnp.int32, (heads, heads), 0) == lax.broadcasted_iota(jnp.int32, (heads, heads), 1)
    exponent = jnp.sum(jnp.where(same, decay[...].astype(F32), 0.0), axis=1, keepdims=True)
    forget = jnp.exp2(-exponent) + spikes[...]
    if wide > length:
        forget = jnp.concatenate([forget, jnp.zeros((heads, wide - length), F32)], axis=1)
    lane = lax.broadcasted_iota(jnp.int32, forget.shape, 1)
    step = 1
    while step < length:
        forget = forget + jnp.where(lane >= step, pltpu.roll(forget, step, 1), 0.0)
        step *= 2
    return forget


def state_sum(left, right, fade):
    return dot((left.T.astype(F32) * fade).astype(BF16), right)


def enter_of(within, h, length):
    return jnp.exp(-within[h : h + 1, :length])


def leave_of(within, h, length):
    return jnp.exp(within[h : h + 1, :length] - within[h : h + 1, length - 1 : length])


def first_kernel(count, heads, decay, spikes, q, k, v, g, *rest):
    payloads, (_, decay_v, spikes_v, left, right, sems) = rest[-6 - len(heads) : -6], rest[-6:]
    place = lax.axis_index("seq")
    length = spikes.shape[1]

    middle = length * 3 // 4 // 128 * 128
    cuts = [slice(0, middle), slice(middle, length)] if middle else [slice(0, length)]
    low = heads[0][0] // 8 * 8
    high = min(-(-(heads[-1][-1] + 1) // 8) * 8, left.shape[1])
    mine = [h for part in heads for h in part]

    def run(a, b, fade_of):
        small = [
            pltpu.make_async_copy(spikes, spikes_v, sems.at[0]),
            pltpu.make_async_copy(decay, decay_v, sems.at[1]),
        ]
        pairs = [
            [
                pltpu.make_async_copy(a.at[cut], left.at[cut], sems.at[2 + 2 * i]),
                pltpu.make_async_copy(b.at[cut], right.at[cut], sems.at[3 + 2 * i]),
            ]
            for i, cut in enumerate(cuts)
        ]
        for copy in sum(pairs, small):
            copy.start()
        for copy in small:
            copy.wait()
        within = running_forget(decay_v, spikes_v)
        fades = {h: fade_of(within, h, length) for h in mine}
        sums = {h: 0.0 for h in mine}
        for cut, pair in zip(cuts, pairs):
            for copy in pair:
                copy.wait()
            a_h = jnp.swapaxes(left[cut, low:high, :], 0, 1)
            b_h = jnp.swapaxes(right[cut, low:high, :], 0, 1)
            for h in mine:
                sums[h] += state_sum(a_h[h - low], b_h[h - low], fades[h][:, cut])
        for part, payload in zip(heads, payloads):
            for i, h in enumerate(part):
                payload[i] = sums[h].astype(BF16)

    @pl.when(place == 0)
    def _():
        run(k, v, leave_of)

    @pl.when(place == count - 1)
    def _():
        run(q, g, enter_of)


def sums_kernel(count, decay, spikes, q, k, v, g, *rest):
    qh, kh, vh, gh, col, row, kv, grad, fade = rest[-16:-7]
    decay_v, spikes_v, *raws, sems = rest[-7:]
    all_heads, length = spikes.shape
    place = lax.axis_index("seq")
    moves = ((spikes, spikes_v), (decay, decay_v), *zip((k, v, q, g), raws))
    copies = [pltpu.make_async_copy(source, target, sems.at[i]) for i, (source, target) in enumerate(moves)]
    for copy in copies:
        copy.start()
    for copy in copies[:2]:
        copy.wait()
    within = running_forget(decay_v, spikes_v)
    row[...] = within[:, None, :]
    fade[...] = jnp.broadcast_to(jnp.exp(-within[:, length - 1 : length])[:, :, None], fade.shape)
    columns = within.T
    for h in range(all_heads):
        col[h] = jnp.broadcast_to(columns[:length, h : h + 1], (length, 128))
    for copy, raw, target in zip(copies[2:], raws, (kh, vh, qh, gh)):
        copy.wait()
        target[...] = jnp.swapaxes(raw[...], 0, 1)

    @pl.when((place > 0) & (place < count - 1))
    def _():
        for h in range(all_heads):
            kv[h] = state_sum(kh[h], vh[h], leave_of(within, h, length)).astype(BF16)
            grad[h] = state_sum(qh[h], gh[h], enter_of(within, h, length)).astype(BF16)


def merge_kernel(count, hop, start, got, kv, grad, fade, *rest):
    payload = rest[-2]
    place = lax.axis_index("seq")
    heads = got.shape[0]
    cut = slice(start, start + heads)
    for at, own in ((hop, kv), (count - 1 - hop, grad)):

        @pl.when(place == at)
        def _():
            payload[...] = (fade[cut] * got[...].astype(F32) + own[cut].astype(F32)).astype(BF16)


def intra_kernel(start, heads, col, row, qh, kh, vh, gh, *rest):
    qg, kg, vg = rest[-4:-1]
    length = qh.shape[1]
    edges = list(range(0, length, 256)) + [length]
    blocks = list(zip(edges[:-1], edges[1:]))

    def one(h, carry):
        q, k, v, g = qh[h], kh[h], vh[h], gh[h]
        qt, gt = q.T, g.T
        scores, probes = {}, {}
        for t0, t1 in blocks:
            for s0, s1 in blocks:
                if s0 > t0:
                    continue
                column = col[h, t0:t1, :]
                if s1 - s0 > 128:
                    column = jnp.concatenate([column, column], axis=1)
                spread = row[h, :, s0:s1] - column[:, : s1 - s0]
                weight = jnp.exp(jnp.minimum(spread, 0.0))
                if s0 == t0:
                    t = lax.broadcasted_iota(jnp.int32, spread.shape, 0)
                    s = lax.broadcasted_iota(jnp.int32, spread.shape, 1)
                    weight = jnp.where(t >= s, weight, 0.0)
                scores[t0, s0] = (dot(q[t0:t1], k[s0:s1], NT) * weight).astype(BF16)
                probes[t0, s0] = (dot(g[t0:t1], v[s0:s1], NT) * weight).astype(BF16)
        for t0, t1 in blocks:
            qg[h, t0:t1, :] = sum(dot(probes[t0, s0], k[s0:s1]) for s0, s1 in blocks if s0 <= t0)
        for s0, s1 in blocks:
            after = [(t0, t1) for t0, t1 in blocks if t0 >= s0]
            kg[h, s0:s1, :] = sum(dot(qt[:, t0:t1], probes[t0, s0]) for t0, t1 in after).T
            vg[h, s0:s1, :] = sum(dot(gt[:, t0:t1], scores[t0, s0]) for t0, t1 in after).T
        return carry

    lax.fori_loop(start, start + heads, one, 0, unroll=max(n for n in range(1, 2 * UNROLL + 1) if heads % n == 0))


def terms(col, kh, vh, gh, state, start, h):
    length = kh.shape[1]

    def leave():
        return jnp.exp(col[h] - col[h, length - 1 : length, :])

    return (
        lambda: jnp.exp(-col[h]) * dot(gh[h], state[h - start], NT),
        lambda: leave() * dot(vh[h], state[h - start], NT),
        lambda: leave() * dot(kh[h], state[h - start]),
    )


def add_terms(which, target, slot, intra, col, kh, vh, gh, state, start, heads):
    def one(i, carry):
        h = start + i
        target[slot, i] = (intra[which][h] + terms(col, kh, vh, gh, state, start, h)[which]()).astype(BF16)
        return carry

    lax.fori_loop(0, heads, one, 0, unroll=min(2 * UNROLL, heads))


def out_copies(tokens, out, sem, parts=2):
    step = tokens.shape[0] // parts
    cuts = [slice(i * step, (i + 1) * step) for i in range(parts)]
    return [(cut, pltpu.make_async_copy(tokens.at[cut], out.at[cut], sem.at[i])) for i, cut in enumerate(cuts)]


def send_out(by_head, tokens, out, sem):
    for cut, copy in out_copies(tokens, out, sem):
        tokens[cut] = jnp.swapaxes(by_head[:, cut, :], 0, 1)
        copy.start()


def wait_out(tokens, out, sem):
    for _, copy in out_copies(tokens, out, sem):
        copy.wait()


def between_kernel(count, sizes, col, kh, vh, gh, qg, kg, vg, *rest):
    hops, chunks = count - 2, len(sizes)
    arrived = rest[: hops * chunks]
    *outs, state, by_head, tokens, sems = rest[-7:]
    intra = (qg, kg, vg)
    all_heads = kh.shape[0]
    place = lax.axis_index("seq")

    def take(end, came_from):
        @pl.when(place == end)
        def _():
            state[...] = jnp.zeros_like(state)

        for hop in range(1, count - 1):

            @pl.when(place == came_from(hop))
            def _():
                at = 0
                for c, heads in enumerate(sizes):
                    state[at : at + heads] = arrived[c * hops + hop - 1][...]
                    at += heads

    def write(which):
        add_terms(which, by_head, which, intra, col, kh, vh, gh, state, 0, all_heads)
        send_out(by_head[which], tokens.at[which], outs[which], sems.at[which])

    @pl.when(place < count - 1)
    def _():
        take(0, lambda hop: hop)
        write(0)

    @pl.when(place > 0)
    def _():
        take(count - 1, lambda hop: count - 1 - hop)
        write(1)
        write(2)

    @pl.when(place < count - 1)
    def _():
        wait_out(tokens.at[0], outs[0], sems.at[0])

    @pl.when(place > 0)
    def _():
        wait_out(tokens.at[1], outs[1], sems.at[1])
        wait_out(tokens.at[2], outs[2], sems.at[2])


def some_heads(parts, starts, low, high, slot):
    pieces = []
    for part, start in zip(parts, starts):
        first, last = max(low - start, 0), min(high - start, part.shape[1])
        if first < last:
            pieces.append(part[slot, first:last])
    return jnp.concatenate(pieces, axis=0)


def ends_kernel(count, starts, c, ready, col, kh, vh, gh, qg, kg, vg, got, *rest):
    by_head, tokens = rest[-2:] if ready else (rest[-1], None)
    parts = [*rest[:c], by_head]
    heads = got.shape[0]
    place = lax.axis_index("seq")
    args = ((qg, kg, vg), col, kh, vh, gh, got, starts[c], heads)

    def lay_out(slot):
        if ready:
            tokens[slot, :, :ready, :] = jnp.swapaxes(some_heads(parts, starts, 0, ready, slot), 0, 1)

    @pl.when(place == count - 1)
    def _():
        add_terms(0, by_head, 0, *args)
        lay_out(0)

    @pl.when(place == 0)
    def _():
        add_terms(1, by_head, 0, *args)
        add_terms(2, by_head, 1, *args)
        lay_out(0)
        lay_out(1)


def last_kernel(count, starts, ready, col, kh, vh, gh, qg, kg, vg, got, *rest):
    *outs, tokens, by_head, sems = rest[-6:]
    parts = [*rest[: len(starts) - 1], by_head]
    all_heads = kh.shape[0]
    place = lax.axis_index("seq")
    args = ((qg, kg, vg), col, kh, vh, gh, got, starts[-1], got.shape[0])

    def write(which, slot):
        add_terms(which, by_head, slot, *args)
        whole = some_heads(parts, starts, ready, all_heads, slot)
        for cut, copy in out_copies(tokens.at[slot], outs[which], sems.at[slot]):
            tokens[slot, cut, ready:, :] = jnp.swapaxes(whole[:, cut, :], 0, 1)
            copy.start()

    @pl.when(place == count - 1)
    def _():
        write(0, 0)
        wait_out(tokens.at[0], outs[0], sems.at[0])

    @pl.when(place == 0)
    def _():
        write(1, 0)
        write(2, 1)
        wait_out(tokens.at[0], outs[1], sems.at[0])
        wait_out(tokens.at[1], outs[2], sems.at[1])


def per_device(count, queries, keys, values, output_gradient, decay_exponent, forget_spikes):
    length, all_heads, size = queries.shape
    chunks = CHUNKS
    sizes = [all_heads // chunks + (c < all_heads % chunks) for c in range(chunks)]
    starts = [sum(sizes[:c]) for c in range(chunks)]
    spikes = forget_spikes.T
    shape = jax.ShapeDtypeStruct
    wide = -(-length // 128) * 128
    by_head = shape((all_heads, length, size), BF16)
    by_head_f = shape((all_heads, length, size), F32)
    states = shape((all_heads, size, size), BF16)
    full = shape(queries.shape, BF16)
    flops = 2 * length * size * size

    def state(c):
        return shape((sizes[c], size, size), BF16)

    def call(kernel, ins, outs, limit, cost, after=(), specs=None, out_spec=VMEM, **more):
        several = isinstance(outs, tuple)
        return pl.pallas_call(
            kernel,
            out_shape=outs,
            in_specs=(specs or [VMEM] * len(ins)) + [ANY] * len(after),
            out_specs=tuple(ANY if o is TOKEN else out_spec for o in outs) if several else out_spec,
            compiler_params=pltpu.CompilerParams(vmem_limit_bytes=limit * MIB),
            cost_estimate=pl.CostEstimate(flops=cost * flops, bytes_accessed=1 << 20, transcendentals=0),
            **more,
        )(*ins, *after)

    tensors = (queries, keys, values, output_gradient)
    raw = pltpu.VMEM(queries.shape, BF16)
    decay = decay_exponent[None, :]
    ranges = [range(a, a + n) for a, n in zip(starts, sizes)]
    payloads = []
    for part in (slice(0, 1), slice(1, chunks)):
        *several, token = call(
            functools.partial(first_kernel, count, ranges[part]),
            (decay, spikes, *tensors),
            (*(pltpu.VMEM((sizes[c], size, size), BF16) for c in range(chunks)[part]), TOKEN),
            FIRST_LIMIT,
            sum(sizes[part]),
            specs=[ANY] * 6,
            scratch_shapes=[
                pltpu.VMEM(decay.shape, jnp.int32),
                pltpu.VMEM(spikes.shape, F32),
                raw,
                raw,
                pltpu.SemaphoreType.DMA((6,)),
            ],
        )
        payloads += several
    qh, kh, vh, gh, col, row, kv, grad, fade = call(
        functools.partial(sums_kernel, count),
        (decay, spikes, *tensors),
        tuple(
            pltpu.VMEM(o.shape, o.dtype)
            for o in (*(by_head,) * 4, by_head_f, shape((all_heads, 1, wide), F32))
            + (states, states, shape((all_heads, 1, size), F32))
        ),
        SUMS_LIMIT,
        2 * all_heads,
        after=payloads[-1:],
        specs=[ANY] * 6,
        scratch_shapes=[
            pltpu.VMEM(decay.shape, jnp.int32),
            pltpu.VMEM(spikes.shape, F32),
            raw,
            raw,
            raw,
            raw,
            pltpu.SemaphoreType.DMA((6,)),
        ],
    )

    intra, placed, done, merged = [], 0, (), ()
    ins = (col, row, qh, kh, vh, gh)

    def span_products(hop, chunk, before=None):
        nonlocal intra, placed, done
        due = all_heads if before is None else all_heads * DUE.get((hop, chunk), 0) // 16
        if due > placed:
            *intra, token = call(
                functools.partial(intra_kernel, placed, due - placed),
                (*ins, *intra),
                (by_head_f,) * 3 + (TOKEN,),
                8,
                5 * (due - placed),
                after=merged if before is None else before,
                input_output_aliases={len(ins) + j: j for j in range(len(intra))},
            )
            placed, done = due, (token,)

    arrived = [[] for _ in range(chunks)]
    span_products(0, 0, ())
    for hop in range(1, count):
        pairs = [(hop - 1, hop), (count - hop, count - hop - 1)]
        for c in range(chunks):
            got = lax.ppermute(payloads[c], "seq", pairs)
            arrived[c].append(got)
            if hop < count - 1:
                payloads[c], *merged = call(
                    functools.partial(merge_kernel, count, hop, starts[c]),
                    (got, kv, grad, fade),
                    (state(c), TOKEN),
                    4,
                    0,
                    after=done,
                )
                done = ()
                span_products(hop, c, merged)
    span_products(0, 0)

    common = (col, kh, vh, gh, *intra)
    came = [a for c in range(chunks) for a in arrived[c][:-1]]
    outs = call(
        functools.partial(between_kernel, count, sizes),
        (*common, *came),
        (full,) * 3,
        16,
        3 * all_heads,
        after=merged,
        out_spec=ANY,
        scratch_shapes=[
            pltpu.VMEM(states.shape, BF16),
            pltpu.VMEM((3,) + by_head.shape, BF16),
            pltpu.VMEM((3,) + full.shape, BF16),
            pltpu.SemaphoreType.DMA((3, 2)),
        ],
    )
    ready = starts[-1] // 8 * 8
    laid = shape((2,) + full.shape, BF16)
    earlier, tokens = [], ()
    for c in range(chunks - 1):
        lays = ready if c == chunks - 2 else 0
        part, *tokens = call(
            functools.partial(ends_kernel, count, starts, c, lays),
            (*common, arrived[c][-1], *earlier),
            (shape((2, sizes[c], length, size), BF16),) + ((laid,) if lays else ()),
            16,
            2 * sizes[c],
        )
        earlier.append(part)
    ins = (*common, arrived[-1][-1], *earlier, *tokens, *outs)
    fixed = len(ins) - 3
    aliases = {fixed + j: j for j in range(3)}
    if tokens:
        aliases[fixed - 1] = 3
    vmem, any_space = [VMEM] * fixed, [ANY] * 3
    *outs, _ = pl.pallas_call(
        functools.partial(last_kernel, count, starts, ready),
        out_shape=(full,) * 3 + (laid,),
        in_specs=vmem + any_space,
        out_specs=(ANY,) * 3 + (VMEM,),
        scratch_shapes=[
            pltpu.VMEM((2, sizes[-1], length, size), BF16),
            pltpu.SemaphoreType.DMA((2, 2)),
        ],
        compiler_params=pltpu.CompilerParams(vmem_limit_bytes=8 * MIB),
        cost_estimate=pl.CostEstimate(flops=2 * sizes[-1] * flops, bytes_accessed=1 << 20, transcendentals=0),
        input_output_aliases=aliases,
    )(*ins)
    return tuple(outs)


def solution(mesh):
    tokens = P(("groups", "seq"), ("head", "sub"), None)
    in_specs = (tokens,) * 4 + (P(("head", "sub")), P(("groups", "seq"), ("head", "sub")))
    return jax.shard_map(
        functools.partial(per_device, mesh.shape["seq"]),
        mesh=mesh,
        in_specs=in_specs,
        out_specs=(tokens,) * 3,
        check_vma=False,
    )
```

```python
import functools

import jax
import jax.numpy as jnp
from jax import lax
from jax.experimental import pallas as pl
from jax.experimental.pallas import tpu as pltpu
from jax.sharding import PartitionSpec as P

VMEM = pl.BlockSpec(memory_space=pltpu.VMEM)
ANY = pl.BlockSpec(memory_space=pl.ANY)
BF16, F32 = jnp.bfloat16, jnp.float32
NT = (((1,), (1,)), ((), ()))
TN = (((0,), (0,)), ((), ()))
NN = (((1,), (0,)), ((), ()))
UNROLL = 4
CHUNKS = 3
FIRST_LIMIT, SUMS_LIMIT = 63, 49
DUE = {(0, 0): 2, (2, 1): 6}
MIB = 2**20
TOKEN = jax.ShapeDtypeStruct((8, 128), F32)


def dot(a, b, dims=NN):
    return lax.dot_general(a, b, dims, preferred_element_type=F32)


def running_forget(decay, spikes):
    heads, length = spikes.shape
    wide = -(-length // 128) * 128
    same = lax.broadcasted_iota(jnp.int32, (heads, heads), 0) == lax.broadcasted_iota(jnp.int32, (heads, heads), 1)
    exponent = jnp.sum(jnp.where(same, decay[...].astype(F32), 0.0), axis=1, keepdims=True)
    forget = jnp.exp2(-exponent) + spikes[...]
    if wide > length:
        forget = jnp.concatenate([forget, jnp.zeros((heads, wide - length), F32)], axis=1)
    lane = lax.broadcasted_iota(jnp.int32, forget.shape, 1)
    step = 1
    while step < length:
        forget = forget + jnp.where(lane >= step, pltpu.roll(forget, step, 1), 0.0)
        step *= 2
    return forget


def state_sum(left, right, fade):
    return dot((left.T.astype(F32) * fade).astype(BF16), right)


def enter_of(within, h, length):
    return jnp.exp(-within[h : h + 1, :length])


def leave_of(within, h, length):
    return jnp.exp(within[h : h + 1, :length] - within[h : h + 1, length - 1 : length])


def first_kernel(count, heads, decay, spikes, q, k, v, g, *rest):
    payloads, (_, decay_v, spikes_v, left, right, sems) = rest[-6 - len(heads) : -6], rest[-6:]
    place = lax.axis_index("seq")
    length = spikes.shape[1]

    middle = length * 3 // 4 // 128 * 128
    cuts = [slice(0, middle), slice(middle, length)] if middle else [slice(0, length)]
    low = heads[0][0] // 8 * 8
    high = min(-(-(heads[-1][-1] + 1) // 8) * 8, left.shape[1])
    mine = [h for part in heads for h in part]

    def run(a, b, fade_of):
        small = [
            pltpu.make_async_copy(spikes, spikes_v, sems.at[0]),
            pltpu.make_async_copy(decay, decay_v, sems.at[1]),
        ]
        pairs = [
            [
                pltpu.make_async_copy(a.at[cut], left.at[cut], sems.at[2 + 2 * i]),
                pltpu.make_async_copy(b.at[cut], right.at[cut], sems.at[3 + 2 * i]),
            ]
            for i, cut in enumerate(cuts)
        ]
        for copy in sum(pairs, small):
            copy.start()
        for copy in small:
            copy.wait()
        within = running_forget(decay_v, spikes_v)
        fades = {h: fade_of(within, h, length) for h in mine}
        sums = {h: 0.0 for h in mine}
        for cut, pair in zip(cuts, pairs):
            for copy in pair:
                copy.wait()
            a_h = jnp.swapaxes(left[cut, low:high, :], 0, 1)
            b_h = jnp.swapaxes(right[cut, low:high, :], 0, 1)
            for h in mine:
                sums[h] += state_sum(a_h[h - low], b_h[h - low], fades[h][:, cut])
        for part, payload in zip(heads, payloads):
            for i, h in enumerate(part):
                payload[i] = sums[h].astype(BF16)

    @pl.when(place == 0)
    def _():
        run(k, v, leave_of)

    @pl.when(place == count - 1)
    def _():
        run(q, g, enter_of)


def sums_kernel(count, decay, spikes, q, k, v, g, *rest):
    qh, kh, vh, gh, col, row, kv, grad, fade = rest[-16:-7]
    decay_v, spikes_v, *raws, sems = rest[-7:]
    all_heads, length = spikes.shape
    place = lax.axis_index("seq")
    moves = ((spikes, spikes_v), (decay, decay_v), *zip((k, v, q, g), raws))
    copies = [pltpu.make_async_copy(source, target, sems.at[i]) for i, (source, target) in enumerate(moves)]
    for copy in copies:
        copy.start()
    for copy in copies[:2]:
        copy.wait()
    within = running_forget(decay_v, spikes_v)
    row[...] = within[:, None, :]
    fade[...] = jnp.broadcast_to(jnp.exp(-within[:, length - 1 : length])[:, :, None], fade.shape)
    columns = within.T
    for h in range(all_heads):
        col[h] = jnp.broadcast_to(columns[:length, h : h + 1], (length, 128))
    for copy, raw, target in zip(copies[2:], raws, (kh, vh, qh, gh)):
        copy.wait()
        target[...] = jnp.swapaxes(raw[...], 0, 1)

    @pl.when((place > 0) & (place < count - 1))
    def _():
        for h in range(all_heads):
            kv[h] = state_sum(kh[h], vh[h], leave_of(within, h, length)).astype(BF16)
            grad[h] = state_sum(qh[h], gh[h], enter_of(within, h, length)).astype(BF16)


def merge_kernel(count, hop, start, got, kv, grad, fade, *rest):
    payload = rest[-2]
    place = lax.axis_index("seq")
    heads = got.shape[0]
    cut = slice(start, start + heads)
    for at, own in ((hop, kv), (count - 1 - hop, grad)):

        @pl.when(place == at)
        def _():
            payload[...] = (fade[cut] * got[...].astype(F32) + own[cut].astype(F32)).astype(BF16)


def intra_kernel(start, heads, col, row, qh, kh, vh, gh, *rest):
    qg, kg, vg = rest[-4:-1]
    length = qh.shape[1]
    edges = list(range(0, length, 256)) + [length]
    blocks = list(zip(edges[:-1], edges[1:]))

    def one(h, carry):
        q, k, v, g = qh[h], kh[h], vh[h], gh[h]
        qt, gt = q.T, g.T
        scores, probes = {}, {}
        for t0, t1 in blocks:
            for s0, s1 in blocks:
                if s0 > t0:
                    continue
                column = col[h, t0:t1, :]
                if s1 - s0 > 128:
                    column = jnp.concatenate([column, column], axis=1)
                spread = row[h, :, s0:s1] - column[:, : s1 - s0]
                weight = jnp.exp(jnp.minimum(spread, 0.0))
                if s0 == t0:
                    t = lax.broadcasted_iota(jnp.int32, spread.shape, 0)
                    s = lax.broadcasted_iota(jnp.int32, spread.shape, 1)
                    weight = jnp.where(t >= s, weight, 0.0)
                scores[t0, s0] = (dot(q[t0:t1], k[s0:s1], NT) * weight).astype(BF16)
                probes[t0, s0] = (dot(g[t0:t1], v[s0:s1], NT) * weight).astype(BF16)
        for t0, t1 in blocks:
            qg[h, t0:t1, :] = sum(dot(probes[t0, s0], k[s0:s1]) for s0, s1 in blocks if s0 <= t0)
        for s0, s1 in blocks:
            after = [(t0, t1) for t0, t1 in blocks if t0 >= s0]
            kg[h, s0:s1, :] = sum(dot(qt[:, t0:t1], probes[t0, s0]) for t0, t1 in after).T
            vg[h, s0:s1, :] = sum(dot(gt[:, t0:t1], scores[t0, s0]) for t0, t1 in after).T
        return carry

    lax.fori_loop(start, start + heads, one, 0, unroll=max(n for n in range(1, 2 * UNROLL + 1) if heads % n == 0))


def terms(col, kh, vh, gh, state, start, h):
    length = kh.shape[1]

    def leave():
        return jnp.exp(col[h] - col[h, length - 1 : length, :])

    return (
        lambda: jnp.exp(-col[h]) * dot(gh[h], state[h - start], NT),
        lambda: leave() * dot(vh[h], state[h - start], NT),
        lambda: leave() * dot(kh[h], state[h - start]),
    )


def add_terms(which, target, slot, intra, col, kh, vh, gh, state, start, heads):
    def one(i, carry):
        h = start + i
        target[slot, i] = (intra[which][h] + terms(col, kh, vh, gh, state, start, h)[which]()).astype(BF16)
        return carry

    lax.fori_loop(0, heads, one, 0, unroll=min(2 * UNROLL, heads))


def out_copies(tokens, out, sem, parts=2):
    step = tokens.shape[0] // parts
    cuts = [slice(i * step, (i + 1) * step) for i in range(parts)]
    return [(cut, pltpu.make_async_copy(tokens.at[cut], out.at[cut], sem.at[i])) for i, cut in enumerate(cuts)]


def send_out(by_head, tokens, out, sem):
    for cut, copy in out_copies(tokens, out, sem):
        tokens[cut] = jnp.swapaxes(by_head[:, cut, :], 0, 1)
        copy.start()


def wait_out(tokens, out, sem):
    for _, copy in out_copies(tokens, out, sem):
        copy.wait()


def between_kernel(count, sizes, col, kh, vh, gh, qg, kg, vg, *rest):
    hops, chunks = count - 2, len(sizes)
    arrived = rest[: hops * chunks]
    *outs, state, by_head, tokens, sems = rest[-7:]
    intra = (qg, kg, vg)
    all_heads = kh.shape[0]
    place = lax.axis_index("seq")

    def take(end, came_from):
        @pl.when(place == end)
        def _():
            state[...] = jnp.zeros_like(state)

        for hop in range(1, count - 1):

            @pl.when(place == came_from(hop))
            def _():
                at = 0
                for c, heads in enumerate(sizes):
                    state[at : at + heads] = arrived[c * hops + hop - 1][...]
                    at += heads

    def write(which):
        add_terms(which, by_head, which, intra, col, kh, vh, gh, state, 0, all_heads)
        send_out(by_head[which], tokens.at[which], outs[which], sems.at[which])

    @pl.when(place < count - 1)
    def _():
        take(0, lambda hop: hop)
        write(0)

    @pl.when(place > 0)
    def _():
        take(count - 1, lambda hop: count - 1 - hop)
        write(1)
        write(2)

    @pl.when(place < count - 1)
    def _():
        wait_out(tokens.at[0], outs[0], sems.at[0])

    @pl.when(place > 0)
    def _():
        wait_out(tokens.at[1], outs[1], sems.at[1])
        wait_out(tokens.at[2], outs[2], sems.at[2])


def some_heads(parts, starts, low, high, slot):
    pieces = []
    for part, start in zip(parts, starts):
        first, last = max(low - start, 0), min(high - start, part.shape[1])
        if first < last:
            pieces.append(part[slot, first:last])
    return jnp.concatenate(pieces, axis=0)


def ends_kernel(count, starts, c, ready, col, kh, vh, gh, qg, kg, vg, got, *rest):
    by_head, tokens = rest[-2:] if ready else (rest[-1], None)
    parts = [*rest[:c], by_head]
    heads = got.shape[0]
    place = lax.axis_index("seq")
    args = ((qg, kg, vg), col, kh, vh, gh, got, starts[c], heads)

    def lay_out(slot):
        if ready:
            tokens[slot, :, :ready, :] = jnp.swapaxes(some_heads(parts, starts, 0, ready, slot), 0, 1)

    @pl.when(place == count - 1)
    def _():
        add_terms(0, by_head, 0, *args)
        lay_out(0)

    @pl.when(place == 0)
    def _():
        add_terms(1, by_head, 0, *args)
        add_terms(2, by_head, 1, *args)
        lay_out(0)
        lay_out(1)


def last_kernel(count, starts, ready, col, kh, vh, gh, qg, kg, vg, got, *rest):
    *outs, tokens, by_head, sems = rest[-6:]
    parts = [*rest[: len(starts) - 1], by_head]
    all_heads = kh.shape[0]
    place = lax.axis_index("seq")
    args = ((qg, kg, vg), col, kh, vh, gh, got, starts[-1], got.shape[0])

    def write(which, slot):
        add_terms(which, by_head, slot, *args)
        whole = some_heads(parts, starts, ready, all_heads, slot)
        for cut, copy in out_copies(tokens.at[slot], outs[which], sems.at[slot]):
            tokens[slot, cut, ready:, :] = jnp.swapaxes(whole[:, cut, :], 0, 1)
            copy.start()

    @pl.when(place == count - 1)
    def _():
        write(0, 0)
        wait_out(tokens.at[0], outs[0], sems.at[0])

    @pl.when(place == 0)
    def _():
        write(1, 0)
        write(2, 1)
        wait_out(tokens.at[0], outs[1], sems.at[0])
        wait_out(tokens.at[1], outs[2], sems.at[1])


def per_device(count, queries, keys, values, output_gradient, decay_exponent, forget_spikes):
    length, all_heads, size = queries.shape
    chunks = CHUNKS
    sizes = [all_heads // chunks + (c < all_heads % chunks) for c in range(chunks)]
    starts = [sum(sizes[:c]) for c in range(chunks)]
    spikes = forget_spikes.T
    shape = jax.ShapeDtypeStruct
    wide = -(-length // 128) * 128
    by_head = shape((all_heads, length, size), BF16)
    by_head_f = shape((all_heads, length, size), F32)
    states = shape((all_heads, size, size), BF16)
    full = shape(queries.shape, BF16)
    flops = 2 * length * size * size

    def state(c):
        return shape((sizes[c], size, size), BF16)

    def call(kernel, ins, outs, limit, cost, after=(), specs=None, out_spec=VMEM, **more):
        several = isinstance(outs, tuple)
        return pl.pallas_call(
            kernel,
            out_shape=outs,
            in_specs=(specs or [VMEM] * len(ins)) + [ANY] * len(after),
            out_specs=tuple(ANY if o is TOKEN else out_spec for o in outs) if several else out_spec,
            compiler_params=pltpu.CompilerParams(vmem_limit_bytes=limit * MIB),
            cost_estimate=pl.CostEstimate(flops=cost * flops, bytes_accessed=1 << 20, transcendentals=0),
            **more,
        )(*ins, *after)

    tensors = (queries, keys, values, output_gradient)
    raw = pltpu.VMEM(queries.shape, BF16)
    decay = decay_exponent[None, :]
    ranges = [range(a, a + n) for a, n in zip(starts, sizes)]
    payloads = []
    for part in (slice(0, 1), slice(1, chunks)):
        *several, token = call(
            functools.partial(first_kernel, count, ranges[part]),
            (decay, spikes, *tensors),
            (*(pltpu.VMEM((sizes[c], size, size), BF16) for c in range(chunks)[part]), TOKEN),
            FIRST_LIMIT,
            sum(sizes[part]),
            specs=[ANY] * 6,
            scratch_shapes=[
                pltpu.VMEM(decay.shape, jnp.int32),
                pltpu.VMEM(spikes.shape, F32),
                raw,
                raw,
                pltpu.SemaphoreType.DMA((6,)),
            ],
        )
        payloads += several
    qh, kh, vh, gh, col, row, kv, grad, fade = call(
        functools.partial(sums_kernel, count),
        (decay, spikes, *tensors),
        tuple(
            pltpu.VMEM(o.shape, o.dtype)
            for o in (*(by_head,) * 4, by_head_f, shape((all_heads, 1, wide), F32))
            + (states, states, shape((all_heads, 1, size), F32))
        ),
        SUMS_LIMIT,
        2 * all_heads,
        after=payloads[-1:],
        specs=[ANY] * 6,
        scratch_shapes=[
            pltpu.VMEM(decay.shape, jnp.int32),
            pltpu.VMEM(spikes.shape, F32),
            raw,
            raw,
            raw,
            raw,
            pltpu.SemaphoreType.DMA((6,)),
        ],
    )

    intra, placed, done, merged = [], 0, (), ()
    ins = (col, row, qh, kh, vh, gh)

    def span_products(hop, chunk, before=None):
        nonlocal intra, placed, done
        due = all_heads if before is None else all_heads * DUE.get((hop, chunk), 0) // 16
        if due > placed:
            *intra, token = call(
                functools.partial(intra_kernel, placed, due - placed),
                (*ins, *intra),
                (by_head_f,) * 3 + (TOKEN,),
                8,
                5 * (due - placed),
                after=merged if before is None else before,
                input_output_aliases={len(ins) + j: j for j in range(len(intra))},
            )
            placed, done = due, (token,)

    arrived = [[] for _ in range(chunks)]
    span_products(0, 0, ())
    for hop in range(1, count):
        pairs = [(hop - 1, hop), (count - hop, count - hop - 1)]
        for c in range(chunks):
            got = lax.ppermute(payloads[c], "seq", pairs)
            arrived[c].append(got)
            if hop < count - 1:
                payloads[c], *merged = call(
                    functools.partial(merge_kernel, count, hop, starts[c]),
                    (got, kv, grad, fade),
                    (state(c), TOKEN),
                    4,
                    0,
                    after=done,
                )
                done = ()
                span_products(hop, c, merged)
    span_products(0, 0)

    common = (col, kh, vh, gh, *intra)
    came = [a for c in range(chunks) for a in arrived[c][:-1]]
    outs = call(
        functools.partial(between_kernel, count, sizes),
        (*common, *came),
        (full,) * 3,
        16,
        3 * all_heads,
        after=merged,
        out_spec=ANY,
        scratch_shapes=[
            pltpu.VMEM(states.shape, BF16),
            pltpu.VMEM((3,) + by_head.shape, BF16),
            pltpu.VMEM((3,) + full.shape, BF16),
            pltpu.SemaphoreType.DMA((3, 2)),
        ],
    )
    ready = starts[-1] // 8 * 8
    laid = shape((2,) + full.shape, BF16)
    earlier, tokens = [], ()
    for c in range(chunks - 1):
        lays = ready if c == chunks - 2 else 0
        part, *tokens = call(
            functools.partial(ends_kernel, count, starts, c, lays),
            (*common, arrived[c][-1], *earlier),
            (shape((2, sizes[c], length, size), BF16),) + ((laid,) if lays else ()),
            16,
            2 * sizes[c],
        )
        earlier.append(part)
    ins = (*common, arrived[-1][-1], *earlier, *tokens, *outs)
    fixed = len(ins) - 3
    aliases = {fixed + j: j for j in range(3)}
    if tokens:
        aliases[fixed - 1] = 3
    vmem, any_space = [VMEM] * fixed, [ANY] * 3
    *outs, _ = pl.pallas_call(
        functools.partial(last_kernel, count, starts, ready),
        out_shape=(full,) * 3 + (laid,),
        in_specs=vmem + any_space,
        out_specs=(ANY,) * 3 + (VMEM,),
        scratch_shapes=[
            pltpu.VMEM((2, sizes[-1], length, size), BF16),
            pltpu.SemaphoreType.DMA((2, 2)),
        ],
        compiler_params=pltpu.CompilerParams(vmem_limit_bytes=8 * MIB),
        cost_estimate=pl.CostEstimate(flops=2 * sizes[-1] * flops, bytes_accessed=1 << 20, transcendentals=0),
        input_output_aliases=aliases,
    )(*ins)
    return tuple(outs)


def solution(mesh):
    tokens = P(("groups", "seq"), ("head", "sub"), None)
    in_specs = (tokens,) * 4 + (P(("head", "sub")), P(("groups", "seq"), ("head", "sub")))
    return jax.shard_map(
        functools.partial(per_device, mesh.shape["seq"]),
        mesh=mesh,
        in_specs=in_specs,
        out_specs=(tokens,) * 3,
        check_vma=False,
    )
```
